128 devices in a mesh: gx: 4 (over z), gy: 32 (over x, y, core).
Axes of the slice: x: 4, y: 4, z: 4, core: 2. Of those that a mesh axis runs over, the one named last changes fastest.
Arguments:
- solid_temp: float32 [128, 1024, 1024], P('gx', 'gy'), may hold values from -6 to 6
- conduct: float32 [128, 1024, 1024], P('gx', 'gy'), may hold values from 0.5 to 4
- power: float32 [128, 1024, 1024], P('gx', 'gy'), may hold values from -6 to 6
- channel_owner: int32 [16384], replicated, may hold values from 0 to 127, as said below
- wall_rows: int32 [524288], P(('gx', 'gy')), may hold values from 0 to 8191, as said below
- span_prop: float32 [2048, 128, 128], P(('gx', 'gy')), as said below
- span_carry: float32 [2048, 128], P(('gx', 'gy')), may hold values from 0.8 to 1
- channel_coef: float32 [32768], P(('gx', 'gy')), may hold values from 0.2 to 2
- channel_inlet: float32 [32768], P(('gx', 'gy')), may hold values from -1 to 1
Outputs:
- solid_out: float32 [128, 1024, 1024], P('gx', 'gy')
- fluid_temp: float32 [32768, 2048], P(('gx', 'gy'))
The draws below stay inside these ranges and needn't reach their ends.
Inputs may be any that keep to these rules, and one draw needn't show every extreme that they name: `channel_owner`: some device owns exactly 256 channels and none more. `wall_rows`: the 4096 entries of one device are distinct rows of that device. `span_prop`: entries [i, j] with i > j are zero.
All inputs are finite; a program needn't handle non-finite values.
Results may differ from the reference program's by a relative error of at most 0.0003.
Values sent between devices are 32-bit elements; how exact they have to be, the bound alone decides.
No kernel may reach another device: no remote copies, remote signals or barrier semaphores. Data moves between devices by JAX's collectives and lax.ppermute only.
A program may use at most 128 MiB of HBM per device.

```python
import math
import jax
import jax.numpy as jnp
from jax import lax

CX = 32
CY = 32
CZ = 1024
BLK = 128
SEG = 16
CH_MEAN = 128
SWEEPS = 2
NX = 128
NY = 1024
NZ = 1024
CHANNELS = 16384
OWN_MAX = 256
CAP = 32
ROWS = 8192
N_GX = 4
N_GY = 32
DEVICES = 128


def draw_channel_owner(key, part):
    key = jax.random.fold_in(key, 11)
    key_pairs, key_sizes, key_order = jax.random.split(key, 3)
    order = jax.random.permutation(key_pairs, DEVICES).astype(jnp.int32)
    extra = jax.random.randint(key_sizes, (DEVICES // 2,), 0, CH_MEAN + 1).astype(jnp.int32)
    extra = extra.at[0].set(CH_MEAN)
    counts = jnp.zeros((DEVICES,), jnp.int32)
    counts = counts.at[order[0::2]].set(CH_MEAN + extra)
    counts = counts.at[order[1::2]].set(CH_MEAN - extra)
    bounds = jnp.cumsum(counts)
    channel = jnp.arange(CHANNELS, dtype=jnp.int32)
    sorted_owner = jnp.sum((bounds[None, :] <= channel[:, None]).astype(jnp.int32), axis=1)
    shuffle = jax.random.permutation(key_order, CHANNELS)
    return sorted_owner[shuffle].astype(jnp.int32)


def draw_wall_rows(key, part):
    key = jax.random.fold_in(key, 23)
    base = jnp.broadcast_to(jnp.arange(ROWS, dtype=jnp.int32), (DEVICES, ROWS))
    mixed = jax.random.permutation(key, base, axis=1, independent=True)
    return mixed[:, :OWN_MAX * SEG].reshape(-1).astype(jnp.int32)


def draw_span_prop(key, part):
    key = jax.random.fold_in(key, 37)
    key_diag, key_off = jax.random.split(key)
    shape = (DEVICES * SEG, BLK, BLK)
    upper = jnp.arange(BLK)[:, None]
    lower = jnp.arange(BLK)[None, :]
    diag = jax.random.uniform(key_diag, shape, jnp.float32, 0.3, 0.6)
    off = 0.04 * jax.random.normal(key_off, shape, jnp.float32)
    values = jnp.where(upper == lower, diag, jnp.where(upper < lower, off, 0.0))
    return values.astype(jnp.float32)


def block_scale(own_key, extent, cuts, low, top_value):
    gain = 1.0
    for dim, parts in cuts:
        draws = jax.random.uniform(jax.random.fold_in(jax.random.fold_in(own_key, 6), dim), (parts,), jnp.float32, low / len(cuts), top_value / len(cuts))
        gain = gain * jnp.repeat(jnp.exp(draws), extent[dim] // parts).reshape((-1,) + (1,) * (len(extent) - 1 - dim))
    return gain


def centred(key, dims, spread, bound, cuts=(), kind=jnp.bfloat16):
    level = block_scale(key, dims, cuts, -0.22, 0.18) if cuts else 1.0
    result = jax.random.normal(key, dims, jnp.float32) * spread * level
    return jnp.minimum(jnp.maximum(result, -bound), bound).astype(kind)


def setup_inputs(seed: int = 0) -> dict:
    splits = jax.random.split(jax.random.key(seed), 10)
    solid_temp = centred(splits[0], (NX, NY, NZ), 1.0, 6.0, ((0, 4), (1, 32)), jnp.float32)
    conduct = jnp.clip(jnp.exp(math.log(4.0) - 2.0794415 * jax.random.uniform(splits[1], (NX, NY, NZ), jnp.float32) ** block_scale(splits[1], (NX, NY, NZ), ((0, 4), (1, 32)), -0.2, 0.2)), 0.5, 4.0)
    power = centred(splits[2], (NX, NY, NZ), 1.0, 6.0, ((0, 4), (1, 32)), jnp.float32)
    channel_owner = draw_channel_owner(jax.random.fold_in(splits[9], 71), 0)
    wall_rows = draw_wall_rows(jax.random.fold_in(splits[9], 71), 0)
    span_prop = draw_span_prop(jax.random.fold_in(splits[9], 71), 0)
    span_carry = jnp.clip(0.8 + 0.19999999 * jax.random.uniform(splits[6], (DEVICES * SEG, BLK), jnp.float32) ** block_scale(splits[6], (DEVICES * SEG, BLK), ((0, 128),), -0.2, 0.2), 0.8, 1.0)
    channel_coef = jnp.clip(jnp.exp(math.log(2.0) - 2.3025851 * jax.random.uniform(splits[7], (DEVICES * OWN_MAX,), jnp.float32) ** block_scale(splits[7], (DEVICES * OWN_MAX,), ((0, 128),), -0.2, 0.2)), 0.2, 2.0)
    channel_inlet = jnp.clip(jax.random.uniform(splits[8], (DEVICES * OWN_MAX,), jnp.float32, -1.0, 1.0) * block_scale(splits[8], (DEVICES * OWN_MAX,), ((0, 128),), -0.4, 0.0), -1.0, 1.0)
    return dict(solid_temp=solid_temp, conduct=conduct, power=power, channel_owner=channel_owner, wall_rows=wall_rows, span_prop=span_prop, span_carry=span_carry, channel_coef=channel_coef, channel_inlet=channel_inlet)


def relax(temp_pad, cond_pad, heat):
    centre = cond_pad[1:-1, 1:-1]
    inner = temp_pad[1:-1, 1:-1]
    numer = heat
    denom = jnp.zeros_like(heat)
    sides = ((cond_pad[2:, 1:-1], temp_pad[2:, 1:-1]), (cond_pad[:-2, 1:-1], temp_pad[:-2, 1:-1]),
             (cond_pad[1:-1, 2:], temp_pad[1:-1, 2:]), (cond_pad[1:-1, :-2], temp_pad[1:-1, :-2]))
    cond_z = jnp.pad(centre, ((0, 0), (0, 0), (1, 1)))
    temp_z = jnp.pad(inner, ((0, 0), (0, 0), (1, 1)))
    sides = sides + ((cond_z[:, :, 2:], temp_z[:, :, 2:]), (cond_z[:, :, :-2], temp_z[:, :, :-2]))
    for cond_side, temp_side in sides:
        face = 0.5 * (centre + cond_side)
        numer = numer + face * temp_side
        denom = denom + face
    denom = denom + jnp.where(centre > 0.0, 0.0, 1.0)
    return jnp.where(centre > 0.0, numer / denom, 0.0)


def reference(solid_temp, conduct, power, channel_owner, wall_rows, span_prop, span_carry, channel_coef, channel_inlet):
    devices = N_GX * N_GY
    rim = ((1, 1), (1, 1), (0, 0))
    cond_pad = jnp.pad(conduct, rim)
    swept = solid_temp
    for sweep in range(SWEEPS):
        swept = relax(jnp.pad(swept, rim), cond_pad, power)
    walls = solid_temp.reshape(N_GX, CX, N_GY, CY, CZ).transpose(0, 2, 1, 3, 4).reshape(devices, ROWS, BLK)
    owners = jnp.arange(devices, dtype=jnp.int32)
    counts = jnp.sum((channel_owner[None, :] == owners[:, None]).astype(jnp.int32), axis=1)
    ticket = jnp.arange(OWN_MAX * SEG, dtype=jnp.int32)[None, :]
    source = (owners[:, None] + ticket) % devices
    place = owners[:, None] * CAP + ticket // devices
    table = wall_rows.reshape(devices, devices * CAP)
    row = table[source, place]
    channel_wall = walls[source, row].reshape(devices, OWN_MAX, SEG, BLK)
    props = span_prop.reshape(devices, SEG, BLK, BLK)
    carries = span_carry.reshape(devices, SEG, BLK)
    coef = channel_coef.reshape(devices, OWN_MAX)
    inlet = channel_inlet.reshape(devices, OWN_MAX)

    def advance(prev, pieces):
        wall_block, prop, carry = pieces
        fresh = jnp.einsum("okb,obc->okc", coef[:, :, None] * wall_block, prop, precision=lax.Precision.HIGHEST)
        fresh = fresh + carry[:, None, :] * prev[:, :, None]
        return fresh[:, :, -1], fresh

    moved = (jnp.moveaxis(channel_wall, 2, 0), jnp.moveaxis(props, 1, 0), jnp.moveaxis(carries, 1, 0))
    last, fluid = lax.scan(advance, inlet, moved)
    fluid = jnp.moveaxis(fluid, 0, 2)
    live = (jnp.arange(OWN_MAX, dtype=jnp.int32)[None, :] < counts[:, None])[:, :, None, None]
    fluid = jnp.where(live, fluid, 0.0)
    flux = jnp.where(live, coef[:, :, None, None] * (channel_wall - fluid), 0.0)
    sink = jnp.zeros_like(walls).at[source, row].add(flux.reshape(devices, OWN_MAX * SEG, BLK))
    sink = sink.reshape(N_GX, N_GY, CX, CY, CZ).transpose(0, 2, 1, 3, 4).reshape(NX, NY, NZ)
    solid_out = swept - sink
    fluid_temp = fluid.reshape(devices * OWN_MAX, SEG * BLK)
    return solid_out, fluid_temp
```

```python
import functools
import jax
import jax.numpy as jnp
from jax import lax
from jax.experimental import pallas as pl
from jax.experimental.pallas import tpu as pltpu
from jax.sharding import PartitionSpec as P

VM = pl.BlockSpec(memory_space=pltpu.VMEM)
SM = pl.BlockSpec(memory_space=pltpu.SMEM)
LIMIT = 56 * 2**20


def tiles(a):
    x, y, z = a.shape
    return a.reshape(x, y // 8, 8, z // 128, 128).transpose(0, 1, 3, 2, 4).reshape(-1, 128)


def untiles(a, x, y, z):
    return a.reshape(x, y // 8, z // 128, 8, 128).transpose(0, 1, 3, 2, 4).reshape(x, y, z)


def gather_kernel(idx, src, out, *, unroll):
    def body(i, _):
        base = pl.multiple_of(i * unroll, unroll)
        at = [idx[base + n] for n in range(unroll)]
        rows = [src[pl.ds(t, 1), :] for t in at]
        for n in range(unroll):
            out[pl.ds(base + n, 1), :] = rows[n]
        return 0
    lax.fori_loop(0, out.shape[0] // unroll, body, 0)


def gather(idx, src, unroll=16):
    return pl.pallas_call(
        functools.partial(gather_kernel, unroll=unroll),
        out_shape=jax.ShapeDtypeStruct((idx.shape[0], 128), jnp.float32),
        in_specs=[SM, VM], out_specs=VM,
        compiler_params=pltpu.CompilerParams(vmem_limit_bytes=LIMIT), name="gather_rows",
    )(idx, src)


def scatter_kernel(idx, rows, src, out, *, unroll):
    out[...] = src[...]
    def body(i, _):
        base = pl.multiple_of(i * unroll, unroll)
        at = [idx[base + n] for n in range(unroll)]
        new = [out[pl.ds(t, 1), :] - rows[pl.ds(base + n, 1), :] for n, t in enumerate(at)]
        for t, v in zip(at, new):
            out[pl.ds(t, 1), :] = v
        return 0
    lax.fori_loop(0, rows.shape[0] // unroll, body, 0)


def scatter(idx, rows, src, unroll=16):
    return pl.pallas_call(
        functools.partial(scatter_kernel, unroll=unroll),
        out_shape=jax.ShapeDtypeStruct(src.shape, jnp.float32),
        in_specs=[SM, VM, VM], out_specs=VM,
        compiler_params=pltpu.CompilerParams(vmem_limit_bytes=LIMIT), name="scatter_rows",
    )(idx, rows, src)


def step_up(a, edge, corner, fill):
    rolled = pltpu.roll(a, 127, 1)
    carried = pltpu.roll(rolled, 7, 0)
    return jnp.where(edge, jnp.where(corner, fill, carried), rolled)


def step_down(a, edge, corner, fill):
    rolled = pltpu.roll(a, 1, 1)
    carried = pltpu.roll(rolled, 1, 0)
    return jnp.where(edge, jnp.where(corner, fill, carried), rolled)


def relax_loop(xs, ys, load_u, load_c, load_p, side_u, side_c, store):
    lane = lax.broadcasted_iota(jnp.int32, (8, 128), 1)
    sub = lax.broadcasted_iota(jnp.int32, (8, 128), 0)
    top, bottom = lane == 127, lane == 0
    last, first = sub == 7, sub == 0

    def body(x, _):
        line = lambda f, side, y: f(x, y) if 0 <= y < ys else side(x, 0 if y < 0 else 1)
        u_old, c_old = line(load_u, side_u, -1), line(load_c, side_c, -1)
        u, c = line(load_u, side_u, 0), line(load_c, side_c, 0)
        w_old, w = u_old * c_old, u * c
        for y in range(ys):
            u_new, c_new = line(load_u, side_u, y + 1), line(load_c, side_c, y + 1)
            w_new = u_new * c_new
            ul, uh = load_u(x - 1, y), load_u(x + 1, y)
            cl, ch = load_c(x - 1, y), load_c(x + 1, y)
            face = c + step_up(c, top, last, 0.0)
            flow = face * step_up(u, top, last, 0.0)
            back = step_down(face * u, bottom, first, 0.0)
            below = step_down(face, bottom, first, c)
            numer = c * ((u_old + u_new) + (ul + uh)) + ((w_old + w_new) + (cl * ul + ch * uh))
            numer = numer + (flow + back) + 2.0 * load_p(x, y)
            denom = 4.0 * c + ((c_old + c_new) + (cl + ch)) + (face + below)
            store(x, y, numer / denom)
            u_old, c_old, w_old = u, c, w
            u, c, w = u_new, c_new, w_new
        return 0

    lax.fori_loop(0, xs, body, 0)


def tile_line(ref, x, y, shift=0):
    return ref[pl.ds(pl.multiple_of((x + shift) * 256, 256) + (y // 8) * 64 + y % 8, 8, stride=8), :]


def sweep1_kernel(u, c, p, xlo, xhi, ylo, yhi, out, fx0, fx1, fy0, fy1, us, cs, ps, sems):
    rows = us.shape[0] - 512
    jobs = [(u, us.at[pl.ds(256, rows)]), (c, cs.at[pl.ds(256, rows)]), (p, ps),
            (xlo.at[pl.ds(0, 256)], us.at[pl.ds(0, 256)]), (xlo.at[pl.ds(256, 256)], cs.at[pl.ds(0, 256)]),
            (xhi.at[pl.ds(0, 256)], us.at[pl.ds(256 + rows, 256)]),
            (xhi.at[pl.ds(256, 256)], cs.at[pl.ds(256 + rows, 256)])]
    copies = [pltpu.make_async_copy(a, b, sems.at[n]) for n, (a, b) in enumerate(jobs)]
    for copy in copies:
        copy.start()
    for copy in copies:
        copy.wait()

    def side(lo, hi, start):
        return lambda x, top: (hi if top else lo)[pl.ds(pl.multiple_of(x * 8 + start, 8), 8), :]

    def store(x, y, v):
        out[pl.ds(pl.multiple_of(x * 256 + y * 8, 8), 8), :] = v
        if y == 0:
            fy0[pl.ds(pl.multiple_of(x * 8, 8), 8), :] = v
        if y == 31:
            fy1[pl.ds(pl.multiple_of(x * 8, 8), 8), :] = v

    relax_loop(32, 32,
               lambda x, y: tile_line(us, x, y, 1), lambda x, y: tile_line(cs, x, y, 1),
               lambda x, y: tile_line(ps, x, y),
               side(ylo, yhi, 0), side(ylo, yhi, 256), store)
    fx0[...] = out[pl.ds(0, 256), :]
    fx1[...] = out[pl.ds(rows - 256, 256), :]


ANY = pl.BlockSpec(memory_space=pl.ANY)


def sweep1(u, c, p, xlo, xhi, ylo, yhi):
    f = jnp.float32
    S = lambda n: jax.ShapeDtypeStruct((n, 128), f)
    return pl.pallas_call(
        sweep1_kernel,
        out_shape=(S(8192), S(256), S(256), S(256), S(256)),
        in_specs=[ANY] * 5 + [VM] * 2, out_specs=(VM,) * 5,
        scratch_shapes=[pltpu.VMEM((8192 + 512, 128), f), pltpu.VMEM((8192 + 512, 128), f),
                        pltpu.VMEM((8192, 128), f), pltpu.SemaphoreType.DMA((7,))],
        compiler_params=pltpu.CompilerParams(vmem_limit_bytes=LIMIT), name="sweep_first",
    )(u, c, p, xlo, xhi, ylo, yhi)


def sweep2_kernel(u, c, p, u_xlo, u_xhi, xlo, xhi, u_ylo, u_yhi, ylo, yhi, out, us, cs, ps, sems):
    rows = us.shape[0] - 512
    jobs = [(u, us.at[pl.ds(256, rows)]), (c, cs.at[pl.ds(256, rows)]), (p, ps),
            (u_xlo, us.at[pl.ds(0, 256)]), (xlo.at[pl.ds(256, 256)], cs.at[pl.ds(0, 256)]),
            (u_xhi, us.at[pl.ds(256 + rows, 256)]),
            (xhi.at[pl.ds(256, 256)], cs.at[pl.ds(256 + rows, 256)])]
    copies = [pltpu.make_async_copy(a, b, sems.at[n]) for n, (a, b) in enumerate(jobs)]
    for copy in copies:
        copy.start()
    for copy in copies:
        copy.wait()

    def side(lo, hi, start):
        return lambda x, top: (hi if top else lo)[pl.ds(pl.multiple_of(x * 8 + start, 8), 8), :]

    def store(x, y, v):
        out[pl.ds(pl.multiple_of(x * 256, 256) + (y // 8) * 64 + y % 8, 8, stride=8), :] = v

    relax_loop(32, 32,
               lambda x, y: us[pl.ds(pl.multiple_of((x + 1) * 256 + y * 8, 8), 8), :],
               lambda x, y: tile_line(cs, x, y, 1), lambda x, y: tile_line(ps, x, y),
               side(u_ylo, u_yhi, 0), side(ylo, yhi, 256), store)


def sweep2(u, c, p, u_xlo, u_xhi, u_ylo, u_yhi, xlo, xhi, ylo, yhi):
    f = jnp.float32
    return pl.pallas_call(
        sweep2_kernel,
        out_shape=jax.ShapeDtypeStruct((8192, 128), f),
        in_specs=[ANY] * 7 + [VM] * 4, out_specs=VM,
        scratch_shapes=[pltpu.VMEM((8192 + 512, 128), f), pltpu.VMEM((8192 + 512, 128), f),
                        pltpu.VMEM((8192, 128), f), pltpu.SemaphoreType.DMA((7,))],
        compiler_params=pltpu.CompilerParams(vmem_limit_bytes=LIMIT), name="sweep_second",
    )(u, c, p, u_xlo, u_xhi, xlo, xhi, u_ylo, u_yhi, ylo, yhi)


def channel_kernel(me, arrived, props, carry, coef, inlet, live, fluid_out, flux_out, prev):
    spans = props.shape[0]
    here = me[0]
    prev[...] = inlet[...]
    bf = jnp.bfloat16
    f = jnp.float32
    keep = live[...] > 0.0

    for s in range(spans):
        starts = [pl.multiple_of(lax.rem(here + (q * 16 + s), 128) * 32, 32) for q in range(8)]
        wall = jnp.concatenate([arrived[pl.ds(b, 32), :] for b in starts], axis=0)
        scale = coef[...]
        x = scale * wall
        hi = x.astype(bf)
        lo = (x - hi.astype(f)).astype(bf)
        p = props[s]
        ph = p.astype(bf)
        pt = (p - ph.astype(f)).astype(bf)
        dot = functools.partial(jnp.dot, preferred_element_type=f)
        fresh = (dot(lo, ph) + dot(hi, pt)) + dot(hi, ph)
        row = carry[pl.ds(s, 1), :]
        before = prev[...]
        fluid = fresh + row * before
        if s + 1 < spans:
            prev[...] = jnp.broadcast_to(fluid[:, 127:128], fluid.shape)
        flux = jnp.where(keep, scale * (wall - fluid), 0.0)
        fluid = jnp.where(keep, fluid, 0.0)
        for q in range(8):
            flux_out[pl.ds(starts[q], 32), :] = flux[q * 32:(q + 1) * 32]
            fluid_out[pl.ds(s * 8 + q, 32, stride=spans * 8), :] = fluid[q * 32:(q + 1) * 32]


def channel(me, arrived, props, carry, coef, inlet, live):
    f = jnp.float32
    return pl.pallas_call(
        channel_kernel,
        out_shape=(jax.ShapeDtypeStruct((4096, 128), f), jax.ShapeDtypeStruct((4096, 128), f)),
        in_specs=[SM] + [VM] * 6, out_specs=(VM, VM),
        scratch_shapes=[pltpu.VMEM((256, 128), f)],
        compiler_params=pltpu.CompilerParams(vmem_limit_bytes=LIMIT), name="channel_march",
    )(me, arrived, props, carry, coef, inlet, live)


def up(a, axis):
    n = lax.axis_size(axis)
    return lax.ppermute(a, axis, [(i, i + 1) for i in range(n - 1)])


def down(a, axis):
    n = lax.axis_size(axis)
    return lax.ppermute(a, axis, [(i + 1, i) for i in range(n - 1)])


def local(solid_temp, conduct, power, channel_owner, wall_rows, span_prop, span_carry,
          channel_coef, channel_inlet):
    both = ("gx", "gy")
    devices = lax.axis_size(both)
    me = lax.axis_index(both)
    nx, ny, nz = solid_temp.shape
    slots = channel_coef.shape[0]
    u, c, p = tiles(solid_temp), tiles(conduct), tiles(power)

    at = (wall_rows & ~63) | ((wall_rows & 7) << 3) | ((wall_rows >> 3) & 7)
    sent = gather(at, u, 32)
    arrived = lax.all_to_all(sent.reshape(devices, -1, 128), both, 0, 0, tiled=True)

    xface = lambda i: jnp.concatenate([u[i * 256:(i + 1) * 256], c[i * 256:(i + 1) * 256]])
    yface = lambda j: jnp.concatenate([a[:, j].reshape(nx * nz // 128, 128) for a in (solid_temp, conduct)])
    xlo, xhi = up(xface(nx - 1), "gx"), down(xface(0), "gx")
    ylo, yhi = up(yface(ny - 1), "gy"), down(yface(0), "gy")
    once, fx0, fx1, fy0, fy1 = sweep1(u, c, p, xlo, xhi, ylo, yhi)
    twice = sweep2(once, c, p, up(fx1, "gx"), down(fx0, "gx"), up(fy1, "gy"), down(fy0, "gy"),
                   xlo, xhi, ylo, yhi)

    owned = jnp.sum((channel_owner == me).astype(jnp.int32))
    turned = lambda v: jnp.broadcast_to(v.reshape(-1, 8).T.reshape(slots, 1), (slots, 128))
    live = turned((jnp.arange(slots, dtype=jnp.int32) < owned).astype(jnp.float32))
    fluid, flux = channel(me.astype(jnp.int32).reshape(1), arrived.reshape(-1, 128), span_prop, span_carry,
                          turned(channel_coef), turned(channel_inlet), live)
    returned = lax.all_to_all(flux.reshape(devices, -1, 128), both, 0, 0, tiled=True)
    solid_out = untiles(scatter(at, returned.reshape(-1, 128), twice, 16), nx, ny, nz)
    return solid_out, untiles(fluid, 1, slots, span_carry.shape[0] * 128)[0]


def solution(mesh):
    both = ("gx", "gy")
    placed = (P("gx", "gy", None),) * 3 + (P(),) + (P(both),) + (
        P(both, None, None), P(both, None), P(both), P(both))
    return jax.shard_map(local, mesh=mesh, in_specs=placed,
                         out_specs=(P("gx", "gy", None), P(both, None)), check_vma=False)
```

```python
import functools

import jax
import jax.numpy as jnp
from jax import lax
from jax.experimental import pallas as pl
from jax.experimental.pallas import tpu as pltpu
from jax.sharding import PartitionSpec as P

F32 = jnp.float32
VM = pl.BlockSpec(memory_space=pltpu.VMEM)
SM = pl.BlockSpec(memory_space=pltpu.SMEM)
ANY = pl.BlockSpec(memory_space=pl.ANY)
PARAMS = pltpu.CompilerParams(vmem_limit_bytes=56 * 2**20)
SMALL = pltpu.CompilerParams(vmem_limit_bytes=16 * 2**20)
LINES = 32
LINE = 8
PLANE = LINES * LINE
ROWS = LINES * PLANE
PARTS = 8
SPAN = ROWS // PARTS


def shape(rows):
    return pltpu.HBM((rows, 128), F32)


def in_hbm(*arrays):
    return [pltpu.with_memory_space_constraint(a, pltpu.HBM) for a in arrays]


def in_smem(*arrays):
    return [pltpu.with_memory_space_constraint(a, pltpu.SMEM) for a in arrays]


def tiles(a):
    x, y, z = a.shape
    return a.reshape(x, y // 8, 8, z // 128, 128).transpose(0, 1, 3, 2, 4).reshape(-1, 128)


def untiles(a, x, y, z):
    return a.reshape(x, y // 8, z // 128, 8, 128).transpose(0, 1, 3, 2, 4).reshape(x, y, z)


def aligned(i, n):
    return pl.multiple_of(i, n)


def tiled_line(x, y):
    return pl.ds(aligned(x * PLANE, PLANE) + (y // 8) * 64 + y % 8, LINE, stride=8)


def plain_line(x, y=0):
    return pl.ds(aligned(x * PLANE + y * LINE, LINE), LINE)


def place_in_tiles(r):
    return (r & ~63) | ((r & 7) << 3) | ((r >> 3) & 7)


def piece(ref, k, shift=0):
    return ref.at[pl.ds(aligned(k * SPAN + shift, 8), SPAN)]


def gather_kernel(rows, u, c, out, at, sx0, sx1, sy0, sy1, block, made, sides, at_v, sems, done, extra):
    loads = [pltpu.make_async_copy(piece(u, k), piece(block, k), sems.at[k]) for k in range(PARTS)]
    lines = [pltpu.make_async_copy(a, b, extra.at[n]) for n, (a, b) in enumerate((
        (c.at[:, pl.ds(0, 64)], sides.at[:, pl.ds(0, 64)]),
        (c.at[:, pl.ds(192, 64)], sides.at[:, pl.ds(192, 64)]),
        (c.at[0, pl.ds(64, 128)], sides.at[0, pl.ds(64, 128)]),
        (c.at[LINES - 1, pl.ds(64, 128)], sides.at[LINES - 1, pl.ds(64, 128)])))]
    for load in loads + lines:
        load.start()
    at_v[...] = place_in_tiles(rows[...])
    listed = pltpu.make_async_copy(at_v, at, sems.at[PARTS])
    listed.start()
    listed.wait()
    for load in loads:
        load.wait()
    groups = rows.shape[0]
    each = groups // PARTS

    def save(k):
        part = pl.ds(aligned(k * each * 128, 128), each * 128)
        return pltpu.make_async_copy(made.at[part], out.at[part], done.at[k])

    def step(k, _):
        def group(i, _):
            g = k * each + i
            base = aligned(g * 128, 128)
            for first in range(0, 128, 32):
                found = [block[pl.ds(at[g, first + n], 1), :] for n in range(32)]
                for n in range(32):
                    made[pl.ds(base + (first + n), 1), :] = found[n]
            return 0

        lax.fori_loop(0, each, group, 0)
        save(k).start()
        return 0

    lax.fori_loop(0, PARTS, step, 0)
    for load in lines:
        load.wait()
    for n in range(LINES):
        row = pl.ds(n * LINE, LINE)
        below = pl.ds(PLANE + n * LINE, LINE)
        for ref, x, y in ((sx0, 0, n), (sx1, LINES - 1, n), (sy0, n, 0), (sy1, n, LINES - 1)):
            ref[row, :] = block[tiled_line(x, y), :]
            ref[below, :] = sides[x, pl.ds((y // 8) * 64 + y % 8, LINE, stride=8), :]
    for k in range(PARTS):
        save(k).wait()


def gather(rows, u, c):
    n = rows.shape[0] * 128
    return pl.pallas_call(
        gather_kernel, out_shape=(shape(n), pltpu.SMEM(rows.shape, jnp.int32)) + (shape(2 * PLANE),) * 4,
        in_specs=[VM, ANY, ANY], out_specs=(ANY, SM) + (VM,) * 4,
        scratch_shapes=[pltpu.VMEM((ROWS, 128), F32), pltpu.VMEM((n, 128), F32), pltpu.VMEM((LINES, PLANE, 128), F32),
                        pltpu.VMEM(rows.shape, jnp.int32), pltpu.SemaphoreType.DMA((PARTS + 1,)),
                        pltpu.SemaphoreType.DMA((PARTS,)), pltpu.SemaphoreType.DMA((4,))],
        compiler_params=PARAMS, name="gather_rows",
    )(rows, *in_hbm(u, c.reshape(LINES, PLANE, 128)))


def finish_kernel(at, flux, src, kx0, kx1, ky0, ky1, xlo, xhi, ylo, yhi, out, block, sides, sems, beside):
    loads = [pltpu.make_async_copy(piece(src, k), piece(block, k), sems.at[k]) for k in range(PARTS)]
    extra = [pltpu.make_async_copy(a, sides.at[n], beside.at[n])
             for n, a in enumerate((kx0, kx1, ky0, ky1, xlo, xhi, ylo, yhi))]
    for load in loads + extra:
        load.start()
    for load in loads:
        load.wait()

    def group(g, _):
        base = aligned(g * 128, 128)
        for first in range(0, 128, 16):
            where = [at[g, first + n] for n in range(16)]
            new = [block[pl.ds(t, 1), :] - flux[pl.ds(base + (first + n), 1), :] for n, t in enumerate(where)]
            for t, v in zip(where, new):
                block[pl.ds(t, 1), :] = v
        return 0

    lax.fori_loop(0, at.shape[0], group, 0)
    for load in extra:
        load.wait()
    for n in range(LINES):
        line = plain_line(0, n)
        for side, place in enumerate((tiled_line(0, n), tiled_line(LINES - 1, n),
                                      tiled_line(n, 0), tiled_line(n, LINES - 1))):
            block[place, :] = block[place, :] + sides[side, line, :] * sides[side + 4, line, :]
    saves = [pltpu.make_async_copy(piece(block, k), piece(out, k), sems.at[k]) for k in range(PARTS)]
    for save in saves:
        save.start()
    for save in saves:
        save.wait()


def finish(at, flux, src, gains, halos):
    return pl.pallas_call(
        finish_kernel, out_shape=shape(ROWS), in_specs=[SM, VM] + [ANY] * 9, out_specs=ANY,
        scratch_shapes=[pltpu.VMEM((ROWS, 128), F32), pltpu.VMEM((8, PLANE, 128), F32),
                        pltpu.SemaphoreType.DMA((PARTS,)), pltpu.SemaphoreType.DMA((8,))],
        compiler_params=SMALL, name="subtract_rows",
    )(*in_smem(at), flux, *in_hbm(src, *gains, *halos))


def step_up(a, edge, corner, fill):
    rolled = pltpu.roll(a, 127, 1)
    carried = pltpu.roll(rolled, 7, 0)
    return jnp.where(edge, jnp.where(corner, fill, carried), rolled)


def step_down(a, edge, corner, fill):
    rolled = pltpu.roll(a, 1, 1)
    carried = pltpu.roll(rolled, 1, 0)
    return jnp.where(edge, jnp.where(corner, fill, carried), rolled)


def relax_plane(x, load_u, load_c, load_p, store, whole):
    lane = lax.broadcasted_iota(jnp.int32, (8, 128), 1)
    sub = lax.broadcasted_iota(jnp.int32, (8, 128), 0)
    top, bottom = lane == 127, lane == 0
    last, first = sub == 7, sub == 0
    zero = jnp.zeros((8, 128), F32)
    u_old, c_old, w_old = zero, zero, zero
    u, c = load_u(x, 0), load_c(x, 0)
    w = u * c
    for y in range(LINES):
        if y + 1 < LINES:
            u_new, c_new = load_u(x, y + 1), load_c(x, y + 1)
            w_new = u_new * c_new
        else:
            u_new, c_new, w_new = zero, zero, zero
        ul, uh = load_u(x - 1, y), load_u(x + 1, y)
        cl, ch = load_c(x - 1, y), load_c(x + 1, y)
        face = c + step_up(c, top, last, 0.0)
        flow = face * step_up(u, top, last, 0.0)
        back = step_down(face * u, bottom, first, 0.0)
        numer = c * ((u_old + u_new) + (ul + uh)) + ((w_old + w_new) + (cl * ul + ch * uh))
        numer = numer + (flow + back) + 2.0 * load_p(x, y)
        denom = None
        if whole:
            below = step_down(face, bottom, first, c)
            denom = 4.0 * c + ((c_old + c_new) + (cl + ch)) + (face + below)
        store(x, y, numer, denom, c)
        u_old, c_old, w_old = u, c, w
        u, c, w = u_new, c_new, w_new


def planes(ready, relax, save):
    each = LINES // PARTS
    ready(0)

    def step(k, _):
        @pl.when(k + 1 < PARTS)
        def _():
            ready(k + 1)

        lax.fori_loop(0, each, lambda i, _: (relax(k * each + i), 0)[1], 0)
        for copy in save(k):
            copy.start()
        return 0

    lax.fori_loop(0, PARTS, step, 0)


def both_sides(relax):
    lax.fori_loop(0, 2, lambda i, _: (relax(i * (LINES - 1)), 0)[1], 0)


def clear_beyond(*refs):
    for ref in refs:
        ref[pl.ds(0, PLANE), :] = jnp.zeros((PLANE, 128), F32)
        ref[pl.ds(PLANE + ROWS, PLANE), :] = jnp.zeros((PLANE, 128), F32)


def first_kernel(after, u, c, p, out, gain, nx0, nx1, ny0, ny1, us, cs, ps, vs, gs, nx, sems, done):
    del after

    def loads(k):
        return [pltpu.make_async_copy(piece(a, k), piece(b, k, shift), sems.at[n, k])
                for n, (a, b, shift) in enumerate(((u, us, PLANE), (c, cs, PLANE), (p, ps, 0)))]

    def save(k):
        return [pltpu.make_async_copy(piece(a, k), piece(b, k), done.at[n, k])
                for n, (a, b) in enumerate(((vs, out), (gs, gain)))]

    for k in range(PARTS):
        for load in loads(k):
            load.start()
    clear_beyond(us, cs)

    def ready(k):
        for load in loads(k):
            load.wait()

    load_u = lambda x, y: us[tiled_line(x + 1, y), :]
    load_c = lambda x, y: cs[tiled_line(x + 1, y), :]
    load_p = lambda x, y: ps[tiled_line(x, y), :]

    def put(sums, start, numer, denom):
        sums[pl.ds(aligned(start, 8), 8), :] = numer
        sums[pl.ds(aligned(start + PLANE, 8), 8), :] = denom

    def store(x, y, numer, denom, c):
        part = 1.0 / denom
        vs[plain_line(x, y), :] = numer * part
        gs[plain_line(x, y), :] = part
        if y == 0:
            put(ny0, x * LINE, numer, denom)
        if y == LINES - 1:
            put(ny1, x * LINE, numer, denom)

    planes(ready, lambda x: relax_plane(x, load_u, load_c, load_p, store, True), save)

    def store_x(x, y, numer, denom, c):
        put(nx, lax.div(x, LINES - 1) * (2 * PLANE) + y * LINE, numer, denom)

    both_sides(lambda x: relax_plane(x, load_u, load_c, load_p, store_x, True))
    nx0[...] = nx[pl.ds(0, 2 * PLANE), :]
    nx1[...] = nx[pl.ds(2 * PLANE, 2 * PLANE), :]
    for k in range(PARTS):
        for copy in save(k):
            copy.wait()


def sweep_first(after, u, c, p):
    return pl.pallas_call(
        first_kernel, out_shape=(shape(ROWS),) * 2 + (shape(2 * PLANE),) * 4,
        in_specs=[ANY] * 4, out_specs=(ANY,) * 2 + (VM,) * 4,
        scratch_shapes=[pltpu.VMEM((ROWS + 2 * PLANE, 128), F32), pltpu.VMEM((ROWS + 2 * PLANE, 128), F32),
                        pltpu.VMEM((ROWS, 128), F32), pltpu.VMEM((ROWS, 128), F32), pltpu.VMEM((ROWS, 128), F32),
                        pltpu.VMEM((4 * PLANE, 128), F32),
                        pltpu.SemaphoreType.DMA((3, PARTS)), pltpu.SemaphoreType.DMA((2, PARTS))],
        compiler_params=PARAMS, name="sweep_first",
    )(*in_hbm(after, u, c, p))


def sides_kernel(sx0, sx1, sy0, sy1, nx0, nx1, ny0, ny1, xlo, xhi, ylo, yhi, fx0, fx1, fy0, fy1):
    def part(ref, start=0):
        return ref[pl.ds(start, PLANE), :]

    def add(numer, denom, c, u_side, c_side):
        return numer + (c + c_side) * u_side, denom + c_side

    for ref, sent, sums, halo, ends in (
        (fx0, sx0, nx0, xlo, ((ylo, 0), (yhi, 0))),
        (fx1, sx1, nx1, xhi, ((ylo, PLANE - 8), (yhi, PLANE - 8))),
        (fy0, sy0, ny0, ylo, ((xlo, 0), (xhi, 0))),
        (fy1, sy1, ny1, yhi, ((xlo, PLANE - 8), (xhi, PLANE - 8))),
    ):
        c = part(sent, PLANE)
        numer, denom = add(part(sums), part(sums, PLANE), c, part(halo), part(halo, PLANE))
        ref[...] = numer / denom
        for rows, (other, line) in zip((0, PLANE - 8), ends):
            at = slice(rows, rows + 8)
            side = other[pl.ds(line, 8), :], other[pl.ds(PLANE + line, 8), :]
            n, d = add(numer[at], denom[at], c[at], *side)
            ref[pl.ds(rows, 8), :] = n / d


def fix_sides(parts, halos):
    return pl.pallas_call(
        sides_kernel, out_shape=(shape(PLANE),) * 4, in_specs=[VM] * 12, out_specs=(VM,) * 4,
        compiler_params=PARAMS, name="sweep_first_sides",
    )(*parts, *halos)


def second_kernel(after, u, c, p, gain, fx0, fx1, fy0, fy1, xlo, xhi, ylo, yhi, out, kx0, kx1, ky0, ky1,
                  us, cs, ps, gs, vs, kx, sems, done):
    del after

    def loads(k):
        return [pltpu.make_async_copy(piece(a, k), piece(b, k, shift), sems.at[n, k])
                for n, (a, b, shift) in enumerate(((u, us, PLANE), (c, cs, PLANE), (p, ps, 0), (gain, gs, 0)))]

    def save(k):
        return [pltpu.make_async_copy(piece(vs, k), piece(out, k), done.at[k])]

    for k in range(PARTS):
        for load in loads(k):
            load.start()
    clear_beyond(us, cs)

    def ready(k):
        for load in loads(k):
            load.wait()
        for i in range(LINES // PARTS):
            x = k * (LINES // PARTS) + i
            us[plain_line(x + 1, 0), :] = fy0[plain_line(0, x), :]
            us[plain_line(x + 1, LINES - 1), :] = fy1[plain_line(0, x), :]

        @pl.when(k == 0)
        def _():
            us[pl.ds(PLANE, PLANE), :] = fx0[...]

        @pl.when(k == PARTS - 1)
        def _():
            us[pl.ds(ROWS, PLANE), :] = fx1[...]

    load_u = lambda x, y: us[plain_line(x + 1, y), :]
    load_c = lambda x, y: cs[tiled_line(x + 1, y), :]
    load_p = lambda x, y: ps[tiled_line(x, y), :]
    y_sides = {0: (ylo, ky0), LINES - 1: (yhi, ky1)}

    def put(x, y, numer, part, c, beside):
        if y in y_sides or beside is not None:
            denom = 1.0 / part
            if beside is not None:
                denom = denom + beside
            if y in y_sides:
                halo, k_side = y_sides[y]
                outer = halo[pl.ds(aligned(PLANE + x * LINE, 8), 8), :]
                part = 1.0 / (denom + outer)
                k_side[plain_line(0, x), :] = (c + outer) * part
            else:
                part = 1.0 / denom
        vs[tiled_line(x, y), :] = numer * part
        return part

    def store(x, y, numer, _, c):
        put(x, y, numer, gs[plain_line(x, y), :], c, None)

    planes(ready, lambda x: relax_plane(x, load_u, load_c, load_p, store, False), lambda k: [])

    def store_x(x, y, numer, _, c):
        line = pl.ds(PLANE + y * LINE, LINE)
        beside = jnp.where(x == 0, xlo[line, :], xhi[line, :])
        part = put(x, y, numer, gs[plain_line(x, y), :], c, beside)
        kx[pl.ds(aligned(lax.div(x, LINES - 1) * PLANE + y * LINE, 8), 8), :] = (c + beside) * part

    both_sides(lambda x: relax_plane(x, load_u, load_c, load_p, store_x, False))
    for k in range(PARTS):
        for copy in save(k):
            copy.start()
    kx0[...] = kx[pl.ds(0, PLANE), :]
    kx1[...] = kx[pl.ds(PLANE, PLANE), :]
    for k in range(PARTS):
        for copy in save(k):
            copy.wait()


def sweep_second(after, u, c, p, gain, faces, halos):
    return pl.pallas_call(
        second_kernel, out_shape=(shape(ROWS),) + (shape(PLANE),) * 4,
        in_specs=[ANY] * 5 + [VM] * 8, out_specs=(ANY,) + (VM,) * 4,
        scratch_shapes=[pltpu.VMEM((ROWS + 2 * PLANE, 128), F32), pltpu.VMEM((ROWS + 2 * PLANE, 128), F32),
                        pltpu.VMEM((ROWS, 128), F32), pltpu.VMEM((ROWS, 128), F32), pltpu.VMEM((ROWS, 128), F32),
                        pltpu.VMEM((2 * PLANE, 128), F32),
                        pltpu.SemaphoreType.DMA((4, PARTS)), pltpu.SemaphoreType.DMA((PARTS,))],
        compiler_params=PARAMS, name="sweep_second",
    )(*in_hbm(after, u, c, p, gain), *faces, *halos)


def channel_kernel(*refs):
    (me, owners, arrived, props, carry, coef_at, inlet_at, fluid_out, flux_out,
     fluids, fluxes, weights, prev, coef, live, done_x, done_f, here_p) = refs[-18:]
    spans, groups = props.shape[0], arrived.shape[0]
    size = arrived.shape[1] // spans
    here = me[0]
    halves = [pltpu.make_async_copy(props.at[part], weights.at[part], here_p.at[n])
              for n, part in enumerate((pl.ds(0, spans // 2), pl.ds(spans // 2, spans // 2)))]
    for load in halves:
        load.start()
    owned = jnp.sum((owners[...] == here).astype(F32), axis=0, keepdims=True)
    owned = jnp.sum(owned, axis=1, keepdims=True)
    bf = jnp.bfloat16
    dot = functools.partial(jnp.dot, preferred_element_type=F32)

    def block(s):
        return pl.ds(aligned(lax.rem(here + s, spans) * size, size), size)

    def save_flux(s):
        return pltpu.make_async_copy(fluxes.at[:, block(s), :], flux_out.at[:, block(s), :], done_x.at[s])

    def save_fluid(n):
        part = pl.ds(n * 4 * groups, 4 * groups)
        return pltpu.make_async_copy(fluids.at[:, part, :], fluid_out.at[:, part, :], done_f.at[n])

    row = lax.broadcasted_iota(jnp.int32, (16, 128), 0)
    lane = lax.broadcasted_iota(jnp.int32, (16, 128), 1)
    for q in range(groups):
        mine = lane == row * groups + q
        for half in range(2):
            part = pl.ds(q * size + half * 16, 16)
            for ref, values in ((prev, inlet_at), (coef, coef_at)):
                column = jnp.sum(jnp.where(mine, values[pl.ds(half, 1), :], 0.0), axis=1, keepdims=True)
                ref[part, :] = jnp.broadcast_to(column, (16, 128))
            live[part, :] = jnp.where(((row + half * 16) * groups + q).astype(F32) < owned, 1.0, 0.0)
    keep = live[...] > 0.0

    for s in range(spans):
        if s % (spans // 2) == 0:
            halves[s // (spans // 2)].wait()
        turn = lax.div(here + s, spans)
        at = [(lax.rem(turn + q, groups), block(s)) for q in range(groups)]
        wall = jnp.concatenate([arrived[g, r, :] for g, r in at], axis=0)
        scale = coef[...]
        x = scale * wall
        hi = x.astype(bf)
        lo = (x - hi.astype(F32)).astype(bf)
        p = weights[s]
        p_hi = p.astype(bf)
        p_lo = (p - p_hi.astype(F32)).astype(bf)
        fresh = (dot(lo, p_hi) + dot(hi, p_lo)) + dot(hi, p_hi)
        fluid = fresh + carry[pl.ds(s, 1), :] * prev[...]
        if s + 1 < spans:
            prev[...] = jnp.broadcast_to(fluid[:, 127:128], fluid.shape)
        flux = jnp.where(keep, scale * (wall - fluid), 0.0)
        fluid = jnp.where(keep, fluid, 0.0)
        for q, (g, r) in enumerate(at):
            fluxes[g, r, :] = flux[q * size:(q + 1) * size]
            fluids[:, s * groups + q, :] = fluid[q * size:(q + 1) * size]
        save_flux(s).start()
        if s % 4 == 3:
            save_fluid(s // 4).start()
    for s in range(spans):
        save_flux(s).wait()
    for n in range(spans // 4):
        save_fluid(n).wait()


def channel(after, me, owners, arrived, props, carry, coef, inlet):
    spans = props.shape[0]
    groups = 8
    size = coef.shape[0] // groups
    rows = spans * size
    fluid, flux = pl.pallas_call(
        channel_kernel,
        out_shape=(jax.ShapeDtypeStruct((size, spans * groups, 128), F32),
                   pltpu.HBM((groups, rows, 128), F32)),
        in_specs=[ANY] * len(after) + [SM] + [VM] * 2 + [ANY] + [VM] * 3, out_specs=(ANY, ANY),
        scratch_shapes=[pltpu.VMEM((size, spans * groups, 128), F32), pltpu.VMEM((groups, rows, 128), F32),
                        pltpu.VMEM(props.shape, F32)]
        + [pltpu.VMEM((groups * size, 128), F32)] * 3
        + [pltpu.SemaphoreType.DMA((spans,)), pltpu.SemaphoreType.DMA((spans // 4,)),
           pltpu.SemaphoreType.DMA((2,))],
        compiler_params=SMALL, name="channel_march",
    )(*in_hbm(*after), me, owners, arrived.reshape(groups, rows, 128), *in_hbm(props), carry,
      coef.reshape(2, 128), inlet.reshape(2, 128))
    return fluid.reshape(-1, 128), flux


def up(a, axis):
    n = lax.axis_size(axis)
    return lax.ppermute(a, axis, [(i, i + 1) for i in range(n - 1)])


def down(a, axis):
    n = lax.axis_size(axis)
    return lax.ppermute(a, axis, [(i + 1, i) for i in range(n - 1)])


def local(solid_temp, conduct, power, channel_owner, wall_rows, span_prop, span_carry,
          channel_coef, channel_inlet):
    both = ("gx", "gy")
    devices = lax.axis_size(both)
    me = lax.axis_index(both).astype(jnp.int32).reshape(1)
    slots = channel_coef.shape[0]
    u, c, p = tiles(solid_temp), tiles(conduct), tiles(power)

    sent, at, *ends = gather(wall_rows.reshape(-1, 128), u, c)
    arrived = lax.all_to_all(sent.reshape(devices, -1, 128), both, 0, 0, tiled=True)

    halos = (up(ends[1], "gx"), down(ends[0], "gx"), up(ends[3], "gy"), down(ends[2], "gy"))
    once, gain, *sums = sweep_first(sent, u, c, p)
    faces = fix_sides((*ends, *sums), halos)

    fluid, flux = channel(faces, me, channel_owner.reshape(-1, 128), arrived, span_prop, span_carry,
                          channel_coef, channel_inlet)
    returned = lax.all_to_all(flux.reshape(devices, -1, 128), both, 0, 0, tiled=True)

    outer = (up(faces[1], "gx"), down(faces[0], "gx"), up(faces[3], "gy"), down(faces[2], "gy"))
    twice, *gains = sweep_second(flux, once, c, p, gain, faces, halos)
    solid_out = finish(at, returned.reshape(-1, 128), twice, gains, outer)
    return untiles(solid_out, *solid_temp.shape), untiles(fluid, 1, slots, span_carry.shape[0] * 128)[0]


def solution(mesh):
    both = ("gx", "gy")
    placed = (P("gx", "gy", None),) * 3 + (P(),) + (P(both),) + (
        P(both, None, None), P(both, None), P(both), P(both))
    return jax.shard_map(local, mesh=mesh, in_specs=placed,
                         out_specs=(P("gx", "gy", None), P(both, None)), check_vma=False)
```

```python
import functools

import jax
import jax.numpy as jnp
from jax import lax
from jax.experimental import pallas as pl
from jax.experimental.pallas import tpu as pltpu
from jax.sharding import PartitionSpec as P

F32 = jnp.float32
VM = pl.BlockSpec(memory_space=pltpu.VMEM)
SM = pl.BlockSpec(memory_space=pltpu.SMEM)
ANY = pl.BlockSpec(memory_space=pl.ANY)
PARAMS = pltpu.CompilerParams(vmem_limit_bytes=56 * 2**20)
SMALL = pltpu.CompilerParams(vmem_limit_bytes=16 * 2**20)
LINES = 32
LINE = 8
PLANE = LINES * LINE
ROWS = LINES * PLANE
PARTS = 8
SPAN = ROWS // PARTS


def shape(rows):
    return pltpu.HBM((rows, 128), F32)


def in_hbm(*arrays):
    return [pltpu.with_memory_space_constraint(a, pltpu.HBM) for a in arrays]


def in_smem(*arrays):
    return [pltpu.with_memory_space_constraint(a, pltpu.SMEM) for a in arrays]


def tiles(a):
    x, y, z = a.shape
    return a.reshape(x, y // 8, 8, z // 128, 128).transpose(0, 1, 3, 2, 4).reshape(-1, 128)


def untiles(a, x, y, z):
    return a.reshape(x, y // 8, z // 128, 8, 128).transpose(0, 1, 3, 2, 4).reshape(x, y, z)


def aligned(i, n):
    return pl.multiple_of(i, n)


def tiled_line(x, y):
    return pl.ds(aligned(x * PLANE, PLANE) + (y // 8) * 64 + y % 8, LINE, stride=8)


def plain_line(x, y=0):
    return pl.ds(aligned(x * PLANE + y * LINE, LINE), LINE)


def place_in_tiles(r):
    return (r & ~63) | ((r & 7) << 3) | ((r >> 3) & 7)


def piece(ref, k, shift=0):
    return ref.at[pl.ds(aligned(k * SPAN + shift, 8), SPAN)]


def gather_kernel(rows, src, out, at, block, made, at_v, sems, done):
    loads = [pltpu.make_async_copy(piece(src, k), piece(block, k), sems.at[k]) for k in range(PARTS)]
    for load in loads:
        load.start()
    at_v[...] = place_in_tiles(rows[...])
    listed = pltpu.make_async_copy(at_v, at, sems.at[PARTS])
    listed.start()
    listed.wait()
    for load in loads:
        load.wait()
    groups = rows.shape[0]
    each = groups // PARTS

    def save(k):
        part = pl.ds(aligned(k * each * 128, 128), each * 128)
        return pltpu.make_async_copy(made.at[part], out.at[part], done.at[k])

    def step(k, _):
        def group(i, _):
            g = k * each + i
            base = aligned(g * 128, 128)
            for first in range(0, 128, 32):
                found = [block[pl.ds(at[g, first + n], 1), :] for n in range(32)]
                for n in range(32):
                    made[pl.ds(base + (first + n), 1), :] = found[n]
            return 0

        lax.fori_loop(0, each, group, 0)
        save(k).start()
        return 0

    lax.fori_loop(0, PARTS, step, 0)
    for k in range(PARTS):
        save(k).wait()


def gather(rows, src):
    n = rows.shape[0] * 128
    return pl.pallas_call(
        gather_kernel, out_shape=(shape(n), pltpu.SMEM(rows.shape, jnp.int32)),
        in_specs=[VM, ANY], out_specs=(ANY, SM),
        scratch_shapes=[pltpu.VMEM((ROWS, 128), F32), pltpu.VMEM((n, 128), F32),
                        pltpu.VMEM(rows.shape, jnp.int32), pltpu.SemaphoreType.DMA((PARTS + 1,)),
                        pltpu.SemaphoreType.DMA((PARTS,))],
        compiler_params=PARAMS, name="gather_rows",
    )(rows, *in_hbm(src))


def finish_kernel(at, flux, src, kx0, kx1, ky0, ky1, xlo, xhi, ylo, yhi, out, block, sink, sides, sems, beside):
    loads = [pltpu.make_async_copy(piece(src, k), piece(block, k), sems.at[k]) for k in range(PARTS)]
    extra = [pltpu.make_async_copy(a, sides.at[n], beside.at[n])
             for n, a in enumerate((kx0, kx1, ky0, ky1, xlo, xhi, ylo, yhi))]
    for load in loads + extra:
        load.start()

    def clear(n, _):
        sink[pl.ds(aligned(n * PLANE, PLANE), PLANE), :] = jnp.zeros((PLANE, 128), F32)
        return 0

    lax.fori_loop(0, LINES, clear, 0)

    def group(g, _):
        base = aligned(g * 128, 128)
        for first in range(0, 128, 16):
            where = [at[g, first + n] for n in range(16)]
            rows = [flux[pl.ds(base + (first + n), 1), :] for n in range(16)]
            for t, v in zip(where, rows):
                sink[pl.ds(t, 1), :] = v
        return 0

    lax.fori_loop(0, at.shape[0], group, 0)
    for load in loads + extra:
        load.wait()
    for n in range(LINES):
        line = plain_line(0, n)
        for side, place in enumerate((tiled_line(0, n), tiled_line(LINES - 1, n),
                                      tiled_line(n, 0), tiled_line(n, LINES - 1))):
            block[place, :] = block[place, :] + sides[side, line, :] * sides[side + 4, line, :]

    def save(k):
        return pltpu.make_async_copy(piece(block, k), piece(out, k), sems.at[k])

    def step(k, _):
        def plane(i, _):
            part = pl.ds(aligned(k * SPAN + i * PLANE, PLANE), PLANE)
            block[part, :] = block[part, :] - sink[part, :]
            return 0

        lax.fori_loop(0, SPAN // PLANE, plane, 0)
        save(k).start()
        return 0

    lax.fori_loop(0, PARTS, step, 0)
    for k in range(PARTS):
        save(k).wait()


def finish(at, flux, src, gains, halos):
    return pl.pallas_call(
        finish_kernel, out_shape=shape(ROWS), in_specs=[SM, VM] + [ANY] * 9, out_specs=ANY,
        scratch_shapes=[pltpu.VMEM((ROWS, 128), F32), pltpu.VMEM((ROWS, 128), F32), pltpu.VMEM((8, PLANE, 128), F32),
                        pltpu.SemaphoreType.DMA((PARTS,)), pltpu.SemaphoreType.DMA((8,))],
        compiler_params=SMALL, name="subtract_rows",
    )(*in_smem(at), flux, *in_hbm(src, *gains, *halos))


def tie_kernel(*refs):
    pass


def after_all(array, others):
    n = len(others)
    return pl.pallas_call(
        tie_kernel, out_shape=pltpu.HBM(array.shape, array.dtype), in_specs=[ANY] * (n + 1), out_specs=ANY,
        input_output_aliases={n: 0}, compiler_params=SMALL, name="tie",
    )(*others, *in_hbm(array))


def step_up(a, edge, corner, fill):
    rolled = pltpu.roll(a, 127, 1)
    carried = pltpu.roll(rolled, 7, 0)
    return jnp.where(edge, jnp.where(corner, fill, carried), rolled)


def step_down(a, edge, corner, fill):
    rolled = pltpu.roll(a, 1, 1)
    carried = pltpu.roll(rolled, 1, 0)
    return jnp.where(edge, jnp.where(corner, fill, carried), rolled)


def relax_plane(x, load_u, load_c, load_p, store, whole):
    lane = lax.broadcasted_iota(jnp.int32, (8, 128), 1)
    sub = lax.broadcasted_iota(jnp.int32, (8, 128), 0)
    top, bottom = lane == 127, lane == 0
    last, first = sub == 7, sub == 0
    zero = jnp.zeros((8, 128), F32)
    u_old, c_old, w_old = zero, zero, zero
    u, c = load_u(x, 0), load_c(x, 0)
    w = u * c
    for y in range(LINES):
        if y + 1 < LINES:
            u_new, c_new = load_u(x, y + 1), load_c(x, y + 1)
            w_new = u_new * c_new
        else:
            u_new, c_new, w_new = zero, zero, zero
        ul, uh = load_u(x - 1, y), load_u(x + 1, y)
        cl, ch = load_c(x - 1, y), load_c(x + 1, y)
        face = c + step_up(c, top, last, 0.0)
        flow = face * step_up(u, top, last, 0.0)
        back = step_down(face * u, bottom, first, 0.0)
        numer = c * ((u_old + u_new) + (ul + uh)) + ((w_old + w_new) + (cl * ul + ch * uh))
        numer = numer + (flow + back) + 2.0 * load_p(x, y)
        denom = None
        if whole:
            below = step_down(face, bottom, first, c)
            denom = 4.0 * c + ((c_old + c_new) + (cl + ch)) + (face + below)
        store(x, y, numer, denom, c)
        u_old, c_old, w_old = u, c, w
        u, c, w = u_new, c_new, w_new


def planes(ready, relax, save):
    each = LINES // PARTS
    ready(0)

    def step(k, _):
        @pl.when(k + 1 < PARTS)
        def _():
            ready(k + 1)

        lax.fori_loop(0, each, lambda i, _: (relax(k * each + i), 0)[1], 0)
        for copy in save(k):
            copy.start()
        return 0

    lax.fori_loop(0, PARTS, step, 0)


def both_sides(relax):
    lax.fori_loop(0, 2, lambda i, _: (relax(i * (LINES - 1)), 0)[1], 0)


def clear_beyond(*refs):
    for ref in refs:
        ref[pl.ds(0, PLANE), :] = jnp.zeros((PLANE, 128), F32)
        ref[pl.ds(PLANE + ROWS, PLANE), :] = jnp.zeros((PLANE, 128), F32)


def first_kernel(after, u, c, p, out, gain, sx0, sx1, sy0, sy1, nx0, nx1, ny0, ny1, us, cs, ps, vs, gs, nx, sems, done):
    del after

    def loads(k):
        return [pltpu.make_async_copy(piece(a, k), piece(b, k, shift), sems.at[n, k])
                for n, (a, b, shift) in enumerate(((u, us, PLANE), (c, cs, PLANE), (p, ps, 0)))]

    def save(k):
        return [pltpu.make_async_copy(piece(a, k), piece(b, k), done.at[n, k])
                for n, (a, b) in enumerate(((vs, out), (gs, gain)))]

    for k in range(PARTS):
        for load in loads(k):
            load.start()
    clear_beyond(us, cs)

    def ready(k):
        for load in loads(k):
            load.wait()

    load_u = lambda x, y: us[tiled_line(x + 1, y), :]
    load_c = lambda x, y: cs[tiled_line(x + 1, y), :]
    load_p = lambda x, y: ps[tiled_line(x, y), :]

    def put(sums, start, numer, denom):
        sums[pl.ds(aligned(start, 8), 8), :] = numer
        sums[pl.ds(aligned(start + PLANE, 8), 8), :] = denom

    def store(x, y, numer, denom, c):
        part = 1.0 / denom
        vs[plain_line(x, y), :] = numer * part
        gs[plain_line(x, y), :] = part
        if y == 0:
            put(ny0, x * LINE, numer, denom)
        if y == LINES - 1:
            put(ny1, x * LINE, numer, denom)

    planes(ready, lambda x: relax_plane(x, load_u, load_c, load_p, store, True), save)

    def store_x(x, y, numer, denom, c):
        put(nx, lax.div(x, LINES - 1) * (2 * PLANE) + y * LINE, numer, denom)

    both_sides(lambda x: relax_plane(x, load_u, load_c, load_p, store_x, True))
    for n in range(LINES):
        row, below = pl.ds(n * LINE, LINE), pl.ds(PLANE + n * LINE, LINE)
        for ref, x, y in ((sx0, 0, n), (sx1, LINES - 1, n), (sy0, n, 0), (sy1, n, LINES - 1)):
            ref[row, :] = load_u(x, y)
            ref[below, :] = load_c(x, y)
    nx0[...] = nx[pl.ds(0, 2 * PLANE), :]
    nx1[...] = nx[pl.ds(2 * PLANE, 2 * PLANE), :]
    for k in range(PARTS):
        for copy in save(k):
            copy.wait()


def sweep_first(after, u, c, p):
    return pl.pallas_call(
        first_kernel, out_shape=(shape(ROWS),) * 2 + (shape(2 * PLANE),) * 8,
        in_specs=[ANY] * 4, out_specs=(ANY,) * 2 + (VM,) * 8,
        scratch_shapes=[pltpu.VMEM((ROWS + 2 * PLANE, 128), F32), pltpu.VMEM((ROWS + 2 * PLANE, 128), F32),
                        pltpu.VMEM((ROWS, 128), F32), pltpu.VMEM((ROWS, 128), F32), pltpu.VMEM((ROWS, 128), F32),
                        pltpu.VMEM((4 * PLANE, 128), F32),
                        pltpu.SemaphoreType.DMA((3, PARTS)), pltpu.SemaphoreType.DMA((2, PARTS))],
        compiler_params=PARAMS, name="sweep_first",
    )(*in_hbm(after, u, c, p))


def sides_kernel(after, sx0, sx1, sy0, sy1, nx0, nx1, ny0, ny1, xlo, xhi, ylo, yhi, fx0, fx1, fy0, fy1):
    del after

    def part(ref, start=0):
        return ref[pl.ds(start, PLANE), :]

    def add(numer, denom, c, u_side, c_side):
        return numer + (c + c_side) * u_side, denom + c_side

    for ref, sent, sums, halo, ends in (
        (fx0, sx0, nx0, xlo, ((ylo, 0), (yhi, 0))),
        (fx1, sx1, nx1, xhi, ((ylo, PLANE - 8), (yhi, PLANE - 8))),
        (fy0, sy0, ny0, ylo, ((xlo, 0), (xhi, 0))),
        (fy1, sy1, ny1, yhi, ((xlo, PLANE - 8), (xhi, PLANE - 8))),
    ):
        c = part(sent, PLANE)
        numer, denom = add(part(sums), part(sums, PLANE), c, part(halo), part(halo, PLANE))
        ref[...] = numer / denom
        for rows, (other, line) in zip((0, PLANE - 8), ends):
            at = slice(rows, rows + 8)
            side = other[pl.ds(line, 8), :], other[pl.ds(PLANE + line, 8), :]
            n, d = add(numer[at], denom[at], c[at], *side)
            ref[pl.ds(rows, 8), :] = n / d


def fix_sides(after, parts, halos):
    return pl.pallas_call(
        sides_kernel, out_shape=(shape(PLANE),) * 4, in_specs=[ANY] + [VM] * 12, out_specs=(VM,) * 4,
        compiler_params=PARAMS, name="sweep_first_sides",
    )(*in_hbm(after), *parts, *halos)


def second_kernel(after, u, c, p, gain, fx0, fx1, fy0, fy1, xlo, xhi, ylo, yhi, out, kx0, kx1, ky0, ky1,
                  us, cs, ps, gs, vs, kx, sems, done):
    del after

    def loads(k):
        return [pltpu.make_async_copy(piece(a, k), piece(b, k, shift), sems.at[n, k])
                for n, (a, b, shift) in enumerate(((u, us, PLANE), (c, cs, PLANE), (p, ps, 0), (gain, gs, 0)))]

    def save(k):
        return [pltpu.make_async_copy(piece(vs, k), piece(out, k), done.at[k])]

    for k in range(PARTS):
        for load in loads(k):
            load.start()
    clear_beyond(us, cs)

    def ready(k):
        for load in loads(k):
            load.wait()
        for i in range(LINES // PARTS):
            x = k * (LINES // PARTS) + i
            us[plain_line(x + 1, 0), :] = fy0[plain_line(0, x), :]
            us[plain_line(x + 1, LINES - 1), :] = fy1[plain_line(0, x), :]

        @pl.when(k == 0)
        def _():
            us[pl.ds(PLANE, PLANE), :] = fx0[...]

        @pl.when(k == PARTS - 1)
        def _():
            us[pl.ds(ROWS, PLANE), :] = fx1[...]

    load_u = lambda x, y: us[plain_line(x + 1, y), :]
    load_c = lambda x, y: cs[tiled_line(x + 1, y), :]
    load_p = lambda x, y: ps[tiled_line(x, y), :]
    y_sides = {0: (ylo, ky0), LINES - 1: (yhi, ky1)}

    def put(x, y, numer, part, c, beside):
        if y in y_sides or beside is not None:
            denom = 1.0 / part
            if beside is not None:
                denom = denom + beside
            if y in y_sides:
                halo, k_side = y_sides[y]
                outer = halo[pl.ds(aligned(PLANE + x * LINE, 8), 8), :]
                part = 1.0 / (denom + outer)
                k_side[plain_line(0, x), :] = (c + outer) * part
            else:
                part = 1.0 / denom
        vs[tiled_line(x, y), :] = numer * part
        return part

    def store(x, y, numer, _, c):
        put(x, y, numer, gs[plain_line(x, y), :], c, None)

    planes(ready, lambda x: relax_plane(x, load_u, load_c, load_p, store, False), lambda k: [])

    def store_x(x, y, numer, _, c):
        line = pl.ds(PLANE + y * LINE, LINE)
        beside = jnp.where(x == 0, xlo[line, :], xhi[line, :])
        part = put(x, y, numer, gs[plain_line(x, y), :], c, beside)
        kx[pl.ds(aligned(lax.div(x, LINES - 1) * PLANE + y * LINE, 8), 8), :] = (c + beside) * part

    both_sides(lambda x: relax_plane(x, load_u, load_c, load_p, store_x, False))
    for k in range(PARTS):
        for copy in save(k):
            copy.start()
    kx0[...] = kx[pl.ds(0, PLANE), :]
    kx1[...] = kx[pl.ds(PLANE, PLANE), :]
    for k in range(PARTS):
        for copy in save(k):
            copy.wait()


def sweep_second(after, u, c, p, gain, faces, halos):
    return pl.pallas_call(
        second_kernel, out_shape=(shape(ROWS),) + (shape(PLANE),) * 4,
        in_specs=[ANY] * 5 + [VM] * 8, out_specs=(ANY,) + (VM,) * 4,
        scratch_shapes=[pltpu.VMEM((ROWS + 2 * PLANE, 128), F32), pltpu.VMEM((ROWS + 2 * PLANE, 128), F32),
                        pltpu.VMEM((ROWS, 128), F32), pltpu.VMEM((ROWS, 128), F32), pltpu.VMEM((ROWS, 128), F32),
                        pltpu.VMEM((2 * PLANE, 128), F32),
                        pltpu.SemaphoreType.DMA((4, PARTS)), pltpu.SemaphoreType.DMA((PARTS,))],
        compiler_params=PARAMS, name="sweep_second",
    )(*in_hbm(after, u, c, p, gain), *faces, *halos)


def channel_kernel(*refs):
    (me, owners, arrived, props, carry, coef_at, inlet_at, fluid_out, flux_out,
     fluids, fluxes, weights, prev, coef, live, done_x, done_f, here_p) = refs[-18:]
    spans, groups = props.shape[0], arrived.shape[0]
    size = arrived.shape[1] // spans
    here = me[0]
    halves = [pltpu.make_async_copy(props.at[part], weights.at[part], here_p.at[n])
              for n, part in enumerate((pl.ds(0, spans // 2), pl.ds(spans // 2, spans // 2)))]
    for load in halves:
        load.start()
    owned = jnp.sum((owners[...] == here).astype(F32), axis=0, keepdims=True)
    owned = jnp.sum(owned, axis=1, keepdims=True)
    bf = jnp.bfloat16
    dot = functools.partial(jnp.dot, preferred_element_type=F32)

    def block(s):
        return pl.ds(aligned(lax.rem(here + s, spans) * size, size), size)

    def save_flux(s):
        return pltpu.make_async_copy(fluxes.at[:, block(s), :], flux_out.at[:, block(s), :], done_x.at[s])

    def save_fluid(n):
        part = pl.ds(n * 4 * groups, 4 * groups)
        return pltpu.make_async_copy(fluids.at[:, part, :], fluid_out.at[:, part, :], done_f.at[n])

    row = lax.broadcasted_iota(jnp.int32, (16, 128), 0)
    lane = lax.broadcasted_iota(jnp.int32, (16, 128), 1)
    for q in range(groups):
        mine = lane == row * groups + q
        for half in range(2):
            part = pl.ds(q * size + half * 16, 16)
            for ref, values in ((prev, inlet_at), (coef, coef_at)):
                column = jnp.sum(jnp.where(mine, values[pl.ds(half, 1), :], 0.0), axis=1, keepdims=True)
                ref[part, :] = jnp.broadcast_to(column, (16, 128))
            live[part, :] = jnp.where(((row + half * 16) * groups + q).astype(F32) < owned, 1.0, 0.0)
    keep = live[...] > 0.0

    for s in range(spans):
        if s % (spans // 2) == 0:
            halves[s // (spans // 2)].wait()
        turn = lax.div(here + s, spans)
        at = [(lax.rem(turn + q, groups), block(s)) for q in range(groups)]
        wall = jnp.concatenate([arrived[g, r, :] for g, r in at], axis=0)
        scale = coef[...]
        x = scale * wall
        hi = x.astype(bf)
        lo = (x - hi.astype(F32)).astype(bf)
        p = weights[s]
        p_hi = p.astype(bf)
        p_lo = (p - p_hi.astype(F32)).astype(bf)
        fresh = (dot(lo, p_hi) + dot(hi, p_lo)) + dot(hi, p_hi)
        fluid = fresh + carry[pl.ds(s, 1), :] * prev[...]
        if s + 1 < spans:
            prev[...] = jnp.broadcast_to(fluid[:, 127:128], fluid.shape)
        flux = jnp.where(keep, scale * (wall - fluid), 0.0)
        fluid = jnp.where(keep, fluid, 0.0)
        for q, (g, r) in enumerate(at):
            fluxes[g, r, :] = flux[q * size:(q + 1) * size]
            fluids[:, s * groups + q, :] = fluid[q * size:(q + 1) * size]
        save_flux(s).start()
        if s % 4 == 3:
            save_fluid(s // 4).start()
    for s in range(spans):
        save_flux(s).wait()
    for n in range(spans // 4):
        save_fluid(n).wait()


def channel(after, me, owners, arrived, props, carry, coef, inlet):
    spans = props.shape[0]
    groups = 8
    size = coef.shape[0] // groups
    rows = spans * size
    fluid, flux = pl.pallas_call(
        channel_kernel,
        out_shape=(jax.ShapeDtypeStruct((size, spans * groups, 128), F32),
                   pltpu.HBM((groups, rows, 128), F32)),
        in_specs=[ANY] * len(after) + [SM] + [VM] * 2 + [ANY] + [VM] * 3, out_specs=(ANY, ANY),
        scratch_shapes=[pltpu.VMEM((size, spans * groups, 128), F32), pltpu.VMEM((groups, rows, 128), F32),
                        pltpu.VMEM(props.shape, F32)]
        + [pltpu.VMEM((groups * size, 128), F32)] * 3
        + [pltpu.SemaphoreType.DMA((spans,)), pltpu.SemaphoreType.DMA((spans // 4,)),
           pltpu.SemaphoreType.DMA((2,))],
        compiler_params=SMALL, name="channel_march",
    )(*in_hbm(*after), me, owners, arrived.reshape(groups, rows, 128), *in_hbm(props), carry,
      coef.reshape(2, 128), inlet.reshape(2, 128))
    return fluid.reshape(-1, 128), flux


def up(a, axis):
    n = lax.axis_size(axis)
    return lax.ppermute(a, axis, [(i, i + 1) for i in range(n - 1)])


def down(a, axis):
    n = lax.axis_size(axis)
    return lax.ppermute(a, axis, [(i + 1, i) for i in range(n - 1)])


def local(solid_temp, conduct, power, channel_owner, wall_rows, span_prop, span_carry,
          channel_coef, channel_inlet):
    both = ("gx", "gy")
    devices = lax.axis_size(both)
    me = lax.axis_index(both).astype(jnp.int32).reshape(1)
    slots = channel_coef.shape[0]
    u, c, p = tiles(solid_temp), tiles(conduct), tiles(power)

    sent, at = gather(wall_rows.reshape(-1, 128), u)
    arrived = lax.all_to_all(sent.reshape(devices, -1, 128), both, 0, 0, tiled=True)

    once, gain, *parts = sweep_first(sent, u, c, p)
    halos = (up(parts[1], "gx"), down(parts[0], "gx"), up(parts[3], "gy"), down(parts[2], "gy"))

    fluid, flux = channel((once,), me, channel_owner.reshape(-1, 128), arrived, span_prop, span_carry,
                          channel_coef, channel_inlet)
    flux = after_all(flux, halos)
    returned = lax.all_to_all(flux.reshape(devices, -1, 128), both, 0, 0, tiled=True)

    faces = fix_sides(flux, parts, halos)
    outer = (up(faces[1], "gx"), down(faces[0], "gx"), up(faces[3], "gy"), down(faces[2], "gy"))
    twice, *gains = sweep_second(flux, once, c, p, gain, faces, halos)
    solid_out = finish(at, returned.reshape(-1, 128), twice, gains, outer)
    return untiles(solid_out, *solid_temp.shape), untiles(fluid, 1, slots, span_carry.shape[0] * 128)[0]


def solution(mesh):
    both = ("gx", "gy")
    placed = (P("gx", "gy", None),) * 3 + (P(),) + (P(both),) + (
        P(both, None, None), P(both, None), P(both), P(both))
    return jax.shard_map(local, mesh=mesh, in_specs=placed,
                         out_specs=(P("gx", "gy", None), P(both, None)), check_vma=False)
```

```python
import functools

import jax
import jax.numpy as jnp
from jax import lax
from jax.experimental import pallas as pl
from jax.experimental.pallas import tpu as pltpu
from jax.sharding import PartitionSpec as P

F32 = jnp.float32
VM = pl.BlockSpec(memory_space=pltpu.VMEM)
SM = pl.BlockSpec(memory_space=pltpu.SMEM)
ANY = pl.BlockSpec(memory_space=pl.ANY)
PARAMS = pltpu.CompilerParams(vmem_limit_bytes=44 * 2**20)
SMALL = pltpu.CompilerParams(vmem_limit_bytes=16 * 2**20)
LINES = 32
LINE = 8
PLANE = LINES * LINE
ROWS = LINES * PLANE
PARTS = 8
FINE = 16
SPAN = ROWS // PARTS


def shape(rows):
    return pltpu.HBM((rows, 128), F32)


def in_hbm(*arrays):
    return [pltpu.with_memory_space_constraint(a, pltpu.HBM) for a in arrays]


def in_vmem(*arrays):
    return [pltpu.with_memory_space_constraint(a, pltpu.VMEM) for a in arrays]


def in_smem(*arrays):
    return [pltpu.with_memory_space_constraint(a, pltpu.SMEM) for a in arrays]


def tiles(a):
    x, y, z = a.shape
    return a.reshape(x, y // 8, 8, z // 128, 128).transpose(0, 1, 3, 2, 4).reshape(-1, 128)


def untiles(a, x, y, z):
    return a.reshape(x, y // 8, z // 128, 8, 128).transpose(0, 1, 3, 2, 4).reshape(x, y, z)


def aligned(i, n):
    return pl.multiple_of(i, n)


def tiled_line(x, y):
    return pl.ds(aligned(x * PLANE, PLANE) + (y // 8) * 64 + y % 8, LINE, stride=8)


def plain_line(x, y=0):
    return pl.ds(aligned(x * PLANE + y * LINE, LINE), LINE)


def place_in_tiles(r):
    return (r & ~63) | ((r & 7) << 3) | ((r >> 3) & 7)


def piece(ref, k, shift=0, parts=PARTS):
    return ref.at[pl.ds(aligned(k * (ROWS // parts) + shift, 8), ROWS // parts)]


def gather_kernel(rows, src, out, at, block, made, at_v, sems, done):
    loads = [pltpu.make_async_copy(piece(src, k), piece(block, k), sems.at[k]) for k in range(PARTS)]
    asked = pltpu.make_async_copy(rows, at_v, sems.at[PARTS])
    asked.start()
    for load in loads:
        load.start()
    asked.wait()
    at_v[...] = place_in_tiles(at_v[...])
    listed = pltpu.make_async_copy(at_v, at, sems.at[PARTS])
    listed.start()
    listed.wait()
    for load in loads:
        load.wait()
    groups = rows.shape[0]
    each = groups // PARTS

    def save(k):
        part = pl.ds(aligned(k * each * 128, 128), each * 128)
        return pltpu.make_async_copy(made.at[part], out.at[part], done.at[k])

    def step(k, _):
        def group(i, _):
            g = k * each + i
            base = aligned(g * 128, 128)
            for first in range(0, 128, 32):
                found = [block[pl.ds(at[g, first + n], 1), :] for n in range(32)]
                for n in range(32):
                    made[pl.ds(base + (first + n), 1), :] = found[n]
            return 0

        lax.fori_loop(0, each, group, 0)
        save(k).start()
        return 0

    lax.fori_loop(0, PARTS, step, 0)
    for k in range(PARTS):
        save(k).wait()


def gather(rows, src):
    n = rows.shape[0] * 128
    return pl.pallas_call(
        gather_kernel, out_shape=(shape(n), pltpu.SMEM(rows.shape, jnp.int32)),
        in_specs=[ANY, ANY], out_specs=(ANY, SM),
        scratch_shapes=[pltpu.VMEM((ROWS, 128), F32), pltpu.VMEM((n, 128), F32),
                        pltpu.VMEM(rows.shape, jnp.int32), pltpu.SemaphoreType.DMA((PARTS + 1,)),
                        pltpu.SemaphoreType.DMA((PARTS,))],
        compiler_params=PARAMS, name="gather_rows",
    )(*in_hbm(rows, src))


def finish_kernel(at, flux, src, kx0, kx1, ky0, ky1, xlo, xhi, ylo, yhi, out, block, sink, sides, sems, beside):
    loads = [pltpu.make_async_copy(piece(src, k), piece(block, k), sems.at[k]) for k in range(PARTS)]
    extra = [pltpu.make_async_copy(a, sides.at[n], beside.at[n])
             for n, a in enumerate((kx0, kx1, ky0, ky1, xlo, xhi, ylo, yhi))]
    for load in loads + extra:
        load.start()

    def clear(n, _):
        sink[pl.ds(aligned(n * PLANE, PLANE), PLANE), :] = jnp.zeros((PLANE, 128), F32)
        return 0

    lax.fori_loop(0, LINES, clear, 0)

    def group(g, _):
        base = aligned(g * 128, 128)
        for first in range(0, 128, 16):
            where = [at[g, first + n] for n in range(16)]
            rows = [flux[pl.ds(base + (first + n), 1), :] for n in range(16)]
            for t, v in zip(where, rows):
                sink[pl.ds(t, 1), :] = v
        return 0

    lax.fori_loop(0, at.shape[0], group, 0)
    for load in loads + extra:
        load.wait()
    for n in range(LINES):
        line = plain_line(0, n)
        for side, place in enumerate((tiled_line(0, n), tiled_line(LINES - 1, n),
                                      tiled_line(n, 0), tiled_line(n, LINES - 1))):
            block[place, :] = block[place, :] + sides[side, line, :] * sides[side + 4, line, :]

    def save(k):
        return pltpu.make_async_copy(piece(block, k), piece(out, k), sems.at[k])

    def step(k, _):
        def plane(i, _):
            part = pl.ds(aligned(k * SPAN + i * PLANE, PLANE), PLANE)
            block[part, :] = block[part, :] - sink[part, :]
            return 0

        lax.fori_loop(0, SPAN // PLANE, plane, 0)
        save(k).start()
        return 0

    lax.fori_loop(0, PARTS, step, 0)
    for k in range(PARTS):
        save(k).wait()


def finish(at, flux, src, gains, halos):
    return pl.pallas_call(
        finish_kernel, out_shape=shape(ROWS), in_specs=[SM, VM] + [ANY] * 9, out_specs=ANY,
        scratch_shapes=[pltpu.VMEM((ROWS, 128), F32), pltpu.VMEM((ROWS, 128), F32), pltpu.VMEM((8, PLANE, 128), F32),
                        pltpu.SemaphoreType.DMA((PARTS,)), pltpu.SemaphoreType.DMA((8,))],
        compiler_params=SMALL, name="subtract_rows",
    )(*in_smem(at), flux, *in_hbm(src, *gains, *halos))


def tie_kernel(*refs):
    pass


def after_all(array, others):
    n = len(others)
    return pl.pallas_call(
        tie_kernel, out_shape=pltpu.HBM(array.shape, array.dtype), in_specs=[VM] * n + [ANY], out_specs=ANY,
        input_output_aliases={n: 0}, compiler_params=SMALL, name="tie",
    )(*in_vmem(*others), *in_hbm(array))


def step_up(a, edge, corner, fill):
    rolled = pltpu.roll(a, 127, 1)
    carried = pltpu.roll(rolled, 7, 0)
    return jnp.where(edge, jnp.where(corner, fill, carried), rolled)


def step_down(a, edge, corner, fill):
    rolled = pltpu.roll(a, 1, 1)
    carried = pltpu.roll(rolled, 1, 0)
    return jnp.where(edge, jnp.where(corner, fill, carried), rolled)


def relax_plane(x, load_u, load_c, load_p, store, whole):
    lane = lax.broadcasted_iota(jnp.int32, (8, 128), 1)
    sub = lax.broadcasted_iota(jnp.int32, (8, 128), 0)
    top, bottom = lane == 127, lane == 0
    last, first = sub == 7, sub == 0
    zero = jnp.zeros((8, 128), F32)
    u_old, c_old, w_old = zero, zero, zero
    u, c = load_u(x, 0), load_c(x, 0)
    w = u * c
    for y in range(LINES):
        if y + 1 < LINES:
            u_new, c_new = load_u(x, y + 1), load_c(x, y + 1)
            w_new = u_new * c_new
        else:
            u_new, c_new, w_new = zero, zero, zero
        ul, uh = load_u(x - 1, y), load_u(x + 1, y)
        cl, ch = load_c(x - 1, y), load_c(x + 1, y)
        face = c + step_up(c, top, last, 0.0)
        flow = face * step_up(u, top, last, 0.0)
        back = step_down(face * u, bottom, first, 0.0)
        numer = c * ((u_old + u_new) + (ul + uh)) + ((w_old + w_new) + (cl * ul + ch * uh))
        numer = numer + (flow + back) + 2.0 * load_p(x, y)
        denom = None
        if whole:
            below = step_down(face, bottom, first, c)
            denom = 4.0 * c + ((c_old + c_new) + (cl + ch)) + (face + below)
        store(x, y, numer, denom, c)
        u_old, c_old, w_old = u, c, w
        u, c, w = u_new, c_new, w_new


def planes(ready, relax, after):
    each = LINES // FINE
    ready(0)

    def step(k, _):
        @pl.when(k + 1 < FINE)
        def _():
            ready(k + 1)

        lax.fori_loop(0, each, lambda i, _: (relax(k * each + i), 0)[1], 0)
        after(k)
        return 0

    lax.fori_loop(0, FINE, step, 0)


def clear_beyond(*refs):
    for ref in refs:
        ref[pl.ds(0, PLANE), :] = jnp.zeros((PLANE, 128), F32)
        ref[pl.ds(PLANE + ROWS, PLANE), :] = jnp.zeros((PLANE, 128), F32)


def first_kernel(after, u, c, p, out, gain, sx0, sx1, sy0, sy1, us, cs, ps, vs, gs, sides, sems, done, sent):
    del after

    def loads(k):
        return [pltpu.make_async_copy(piece(a, k, 0, FINE), piece(b, k, shift, FINE), sems.at[n, k])
                for n, (a, b, shift) in enumerate(((u, us, PLANE), (c, cs, PLANE), (p, ps, 0)))]

    def saves(k):
        return [pltpu.make_async_copy(piece(a, k, 0, FINE), piece(b, k, 0, FINE), done.at[n, k])
                for n, (a, b) in enumerate(((vs, out), (gs, gain)))]

    for k in range(FINE):
        for load in loads(k):
            load.start()
    clear_beyond(us, cs)

    load_u = lambda x, y: us[tiled_line(x + 1, y), :]
    load_c = lambda x, y: cs[tiled_line(x + 1, y), :]
    load_p = lambda x, y: ps[tiled_line(x, y), :]
    sends = [pltpu.make_async_copy(sides.at[n], ref, sent.at[n]) for n, ref in enumerate((sx0, sx1, sy0, sy1))]

    def ready(k):
        for load in loads(k):
            load.wait()

        @pl.when(k == FINE - 1)
        def _():
            for n in range(LINES):
                row, below = pl.ds(n * LINE, LINE), pl.ds(PLANE + n * LINE, LINE)
                for side, (x, y) in enumerate(((0, n), (LINES - 1, n), (n, 0), (n, LINES - 1))):
                    sides[side, row, :] = load_u(x, y)
                    sides[side, below, :] = load_c(x, y)
            for send in sends:
                send.start()

    def store(x, y, numer, denom, c):
        part = 1.0 / denom
        vs[plain_line(x, y), :] = numer * part
        gs[plain_line(x, y), :] = part

    def after_piece(k):
        for save in saves(k):
            save.start()

    planes(ready, lambda x: relax_plane(x, load_u, load_c, load_p, store, True), after_piece)
    for send in sends:
        send.wait()
    for k in range(FINE):
        for save in saves(k):
            save.wait()


def sweep_first(after, u, c, p):
    return pl.pallas_call(
        first_kernel, out_shape=(shape(ROWS),) * 2 + (shape(2 * PLANE),) * 4,
        in_specs=[ANY] * 4, out_specs=(ANY,) * 6,
        scratch_shapes=[pltpu.VMEM((ROWS + 2 * PLANE, 128), F32), pltpu.VMEM((ROWS + 2 * PLANE, 128), F32),
                        pltpu.VMEM((ROWS, 128), F32), pltpu.VMEM((ROWS, 128), F32), pltpu.VMEM((ROWS, 128), F32),
                        pltpu.VMEM((4, 2 * PLANE, 128), F32), pltpu.SemaphoreType.DMA((3, FINE)),
                        pltpu.SemaphoreType.DMA((2, FINE)), pltpu.SemaphoreType.DMA((4,))],
        compiler_params=PARAMS, name="sweep_first",
    )(*in_hbm(after, u, c, p))


def sides_kernel(after, once, gain, sx0, sx1, sy0, sy1, xlo, xhi, ylo, yhi, fx0, fx1, fy0, fy1,
                 bx0, bx1, by0, by1, on_x, on_y, cs, sems, passed):
    del after
    copies = []
    for n, a in enumerate((once, gain)):
        for side, x in enumerate((0, LINES - 1)):
            copies.append((a.at[x], on_x.at[n, side]))
            copies.append((a.at[:, pl.ds(x * LINE, LINE)], on_y.at[n, side]))
    for side, a in enumerate((sx0, sx1, sy0, sy1)):
        copies.append((a.at[pl.ds(PLANE, PLANE)], cs.at[side]))
    copies = [pltpu.make_async_copy(a, b, sems.at[n]) for n, (a, b) in enumerate(copies)]
    for copy in copies:
        copy.start()
    passing = [pltpu.make_async_copy(a.at[pl.ds(PLANE, PLANE)], b, passed.at[n])
               for n, (a, b) in enumerate(((xlo, bx0), (xhi, bx1), (ylo, by0), (yhi, by1)))]
    for copy in passing:
        copy.start()
    for copy in copies:
        copy.wait()
    end = PLANE - LINE
    for side, (ref, halo, ends) in enumerate((
        (fx0, xlo, ((ylo, 0), (yhi, 0))), (fx1, xhi, ((ylo, end), (yhi, end))),
        (fy0, ylo, ((xlo, 0), (xhi, 0))), (fy1, yhi, ((xlo, end), (xhi, end))),
    )):
        c = cs[side]
        v, g = [on_x[n, side] if side < 2 else on_y[n, side - 2].reshape(PLANE, 128) for n in range(2)]
        c_out = halo[pl.ds(PLANE, PLANE), :]
        numer = v + g * ((c + c_out) * halo[pl.ds(0, PLANE), :])
        denom = 1.0 + g * c_out
        ref[...] = numer / denom
        for start, (other, line) in zip((0, end), ends):
            at = slice(start, start + LINE)
            c_out = other[pl.ds(PLANE + line, LINE), :]
            more = numer[at] + g[at] * ((c[at] + c_out) * other[pl.ds(line, LINE), :])
            ref[pl.ds(start, LINE), :] = more / (denom[at] + g[at] * c_out)
    for copy in passing:
        copy.wait()


def fix_sides(after, once, gain, sides, halos):
    by_plane = lambda a: a.reshape(LINES, PLANE, 128)
    return pl.pallas_call(
        sides_kernel, out_shape=(shape(PLANE),) * 8, in_specs=[ANY] * 7 + [VM] * 4, out_specs=(VM,) * 4 + (ANY,) * 4,
        scratch_shapes=[pltpu.VMEM((2, 2, PLANE, 128), F32), pltpu.VMEM((2, 2, LINES, LINE, 128), F32),
                        pltpu.VMEM((4, PLANE, 128), F32), pltpu.SemaphoreType.DMA((12,)), pltpu.SemaphoreType.DMA((4,))],
        compiler_params=SMALL, name="sweep_first_sides",
    )(*in_hbm(after, by_plane(once), by_plane(gain), *sides), *in_vmem(*halos))


def second_kernel(after, u, c, p, gain, fx0, fx1, fy0, fy1, xlo, xhi, ylo, yhi, out, kx0, kx1, ky0, ky1,
                  us, cs, ps, gs, vs, sems, done):
    del after

    def loads(k):
        return [pltpu.make_async_copy(piece(a, k, 0, FINE), piece(b, k, shift, FINE), sems.at[n, k])
                for n, (a, b, shift) in enumerate(((u, us, PLANE), (c, cs, PLANE), (p, ps, 0), (gain, gs, 0)))]

    def save(k):
        return pltpu.make_async_copy(piece(vs, k, 0, FINE), piece(out, k, 0, FINE), done.at[k])

    for k in range(FINE):
        for load in loads(k):
            load.start()
    clear_beyond(us, cs)

    def ready(k):
        for load in loads(k):
            load.wait()
        for i in range(LINES // FINE):
            x = k * (LINES // FINE) + i
            us[plain_line(x + 1, 0), :] = fy0[plain_line(0, x), :]
            us[plain_line(x + 1, LINES - 1), :] = fy1[plain_line(0, x), :]

        @pl.when(k == 0)
        def _():
            us[pl.ds(PLANE, PLANE), :] = fx0[...]

        @pl.when(k == FINE - 1)
        def _():
            us[pl.ds(ROWS, PLANE), :] = fx1[...]

    load_u = lambda x, y: us[plain_line(x + 1, y), :]
    load_c = lambda x, y: cs[tiled_line(x + 1, y), :]
    load_p = lambda x, y: ps[tiled_line(x, y), :]
    y_sides = {0: (ylo, ky0), LINES - 1: (yhi, ky1)}

    def beyond_y(x, y, part):
        outer = y_sides[y][0][plain_line(0, x), :]
        return outer, part / (1.0 + part * outer)

    def store(x, y, numer, _, c):
        part = gs[plain_line(x, y), :]
        if y in y_sides:
            outer, part = beyond_y(x, y, part)
            y_sides[y][1][plain_line(0, x), :] = (c + outer) * part
        vs[tiled_line(x, y), :] = numer * part

    def x_side(x, halo, k_side):
        for y in range(LINES):
            line = pl.ds(y * LINE, LINE)
            outer = halo[pl.ds(y * LINE, LINE), :]
            part = gs[plain_line(x, y), :]
            if y in y_sides:
                part = beyond_y(x, y, part)[1]
            less = 1.0 / (1.0 + part * outer)
            if y in y_sides:
                k_y = y_sides[y][1]
                k_y[plain_line(0, x), :] = k_y[plain_line(0, x), :] * less
            vs[tiled_line(x, y), :] = vs[tiled_line(x, y), :] * less
            k_side[line, :] = (load_c(x, y) + outer) * (part * less)

    def after_piece(k):
        @pl.when(k == 0)
        def _():
            x_side(0, xlo, kx0)

        @pl.when(k == FINE - 1)
        def _():
            x_side(LINES - 1, xhi, kx1)

        save(k).start()

    planes(ready, lambda x: relax_plane(x, load_u, load_c, load_p, store, False), after_piece)
    for k in range(FINE):
        save(k).wait()


def sweep_second(after, u, c, p, gain, faces, beyond):
    return pl.pallas_call(
        second_kernel, out_shape=(shape(ROWS),) + (shape(PLANE),) * 4,
        in_specs=[ANY] * 5 + [VM] * 8, out_specs=(ANY,) + (VM,) * 4,
        scratch_shapes=[pltpu.VMEM((ROWS + 2 * PLANE, 128), F32), pltpu.VMEM((ROWS + 2 * PLANE, 128), F32),
                        pltpu.VMEM((ROWS, 128), F32), pltpu.VMEM((ROWS, 128), F32), pltpu.VMEM((ROWS, 128), F32),
                        pltpu.SemaphoreType.DMA((4, FINE)), pltpu.SemaphoreType.DMA((FINE,))],
        compiler_params=PARAMS, name="sweep_second",
    )(*in_hbm(after, u, c, p, gain, *faces, *beyond))


def channel_kernel(*refs):
    (me, owners, arrived, props, carry, coef_at, inlet_at, fluid_out, flux_out,
     fluids, fluxes, weights, prev, coef, live, done_x, done_f, here_p) = refs[-18:]
    spans, groups = props.shape[0], arrived.shape[0]
    size = arrived.shape[1] // spans
    here = me[0]
    halves = [pltpu.make_async_copy(props.at[part], weights.at[part], here_p.at[n])
              for n, part in enumerate((pl.ds(0, spans // 2), pl.ds(spans // 2, spans // 2)))]
    for load in halves:
        load.start()
    owned = jnp.sum((owners[...] == here).astype(F32), axis=0, keepdims=True)
    owned = jnp.sum(owned, axis=1, keepdims=True)
    bf = jnp.bfloat16
    dot = functools.partial(jnp.dot, preferred_element_type=F32)

    def block(s):
        return pl.ds(aligned(lax.rem(here + s, spans) * size, size), size)

    def save_flux(s):
        return pltpu.make_async_copy(fluxes.at[:, block(s), :], flux_out.at[:, block(s), :], done_x.at[s])

    def save_fluid(n):
        part = pl.ds(n * 4 * groups, 4 * groups)
        return pltpu.make_async_copy(fluids.at[:, part, :], fluid_out.at[:, part, :], done_f.at[n])

    row = lax.broadcasted_iota(jnp.int32, (16, 128), 0)
    lane = lax.broadcasted_iota(jnp.int32, (16, 128), 1)
    for q in range(groups):
        mine = lane == row * groups + q
        for half in range(2):
            part = pl.ds(q * size + half * 16, 16)
            for ref, values in ((prev, inlet_at), (coef, coef_at)):
                column = jnp.sum(jnp.where(mine, values[pl.ds(half, 1), :], 0.0), axis=1, keepdims=True)
                ref[part, :] = jnp.broadcast_to(column, (16, 128))
            live[part, :] = jnp.where(((row + half * 16) * groups + q).astype(F32) < owned, 1.0, 0.0)
    keep = live[...] > 0.0

    for s in range(spans):
        if s % (spans // 2) == 0:
            halves[s // (spans // 2)].wait()
        turn = lax.div(here + s, spans)
        at = [(lax.rem(turn + q, groups), block(s)) for q in range(groups)]
        wall = jnp.concatenate([arrived[g, r, :] for g, r in at], axis=0)
        scale = coef[...]
        x = scale * wall
        hi = x.astype(bf)
        lo = (x - hi.astype(F32)).astype(bf)
        p = weights[s]
        p_hi = p.astype(bf)
        p_lo = (p - p_hi.astype(F32)).astype(bf)
        fresh = (dot(lo, p_hi) + dot(hi, p_lo)) + dot(hi, p_hi)
        fluid = fresh + carry[pl.ds(s, 1), :] * prev[...]
        if s + 1 < spans:
            prev[...] = jnp.broadcast_to(fluid[:, 127:128], fluid.shape)
        flux = jnp.where(keep, scale * (wall - fluid), 0.0)
        fluid = jnp.where(keep, fluid, 0.0)
        for q, (g, r) in enumerate(at):
            fluxes[g, r, :] = flux[q * size:(q + 1) * size]
            fluids[:, s * groups + q, :] = fluid[q * size:(q + 1) * size]
        save_flux(s).start()
        if s % 4 == 3:
            save_fluid(s // 4).start()
    for s in range(spans):
        save_flux(s).wait()
    for n in range(spans // 4):
        save_fluid(n).wait()


def channel(after, me, owners, arrived, props, carry, coef, inlet):
    spans = props.shape[0]
    groups = 8
    size = coef.shape[0] // groups
    rows = spans * size
    fluid, flux = pl.pallas_call(
        channel_kernel,
        out_shape=(jax.ShapeDtypeStruct((size, spans * groups, 128), F32),
                   pltpu.HBM((groups, rows, 128), F32)),
        in_specs=[ANY] * len(after) + [SM] + [VM] * 2 + [ANY] + [VM] * 3, out_specs=(ANY, ANY),
        scratch_shapes=[pltpu.VMEM((size, (spans + 1) * groups, 128), F32), pltpu.VMEM((groups, rows, 128), F32),
                        pltpu.VMEM(props.shape, F32)]
        + [pltpu.VMEM((groups * size, 128), F32)] * 3
        + [pltpu.SemaphoreType.DMA((spans,)), pltpu.SemaphoreType.DMA((spans // 4,)),
           pltpu.SemaphoreType.DMA((2,))],
        compiler_params=SMALL, name="channel_march",
    )(*in_hbm(*after), me, owners, arrived.reshape(groups, rows, 128), *in_hbm(props), carry,
      coef.reshape(2, 128), inlet.reshape(2, 128))
    return fluid.reshape(-1, 128), flux


def up(a, axis):
    n = lax.axis_size(axis)
    return lax.ppermute(a, axis, [(i, i + 1) for i in range(n - 1)])


def down(a, axis):
    n = lax.axis_size(axis)
    return lax.ppermute(a, axis, [(i + 1, i) for i in range(n - 1)])


def local(solid_temp, conduct, power, channel_owner, wall_rows, span_prop, span_carry,
          channel_coef, channel_inlet):
    both = ("gx", "gy")
    devices = lax.axis_size(both)
    me = lax.axis_index(both).astype(jnp.int32).reshape(1)
    slots = channel_coef.shape[0]
    u, c, p = tiles(solid_temp), tiles(conduct), tiles(power)

    sent, at = gather(wall_rows.reshape(-1, 128), u)
    arrived = lax.all_to_all(sent.reshape(devices, -1, 128), both, 0, 0, tiled=True)

    once, gain, *sides = sweep_first(sent, u, c, p)
    halos = (up(sides[1], "gx"), down(sides[0], "gx"), up(sides[3], "gy"), down(sides[2], "gy"))

    fluid, flux = channel((once,), me, channel_owner.reshape(-1, 128), arrived, span_prop, span_carry,
                          channel_coef, channel_inlet)
    flux = after_all(flux, halos)
    returned = lax.all_to_all(flux.reshape(devices, -1, 128), both, 0, 0, tiled=True)

    faces = fix_sides(flux, once, gain, sides, halos)
    faces, beyond = faces[:4], faces[4:]
    outer = (up(faces[1], "gx"), down(faces[0], "gx"), up(faces[3], "gy"), down(faces[2], "gy"))
    twice, *gains = sweep_second(flux, once, c, p, gain, faces, beyond)
    solid_out = finish(at, returned.reshape(-1, 128), twice, gains, outer)
    return untiles(solid_out, *solid_temp.shape), untiles(fluid, 1, slots, span_carry.shape[0] * 128)[0]


def solution(mesh):
    both = ("gx", "gy")
    placed = (P("gx", "gy", None),) * 3 + (P(),) + (P(both),) + (
        P(both, None, None), P(both, None), P(both), P(both))
    return jax.shard_map(local, mesh=mesh, in_specs=placed,
                         out_specs=(P("gx", "gy", None), P(both, None)), check_vma=False)
```

```python
import functools

import jax
import jax.numpy as jnp
from jax import lax
from jax.experimental import pallas as pl
from jax.experimental.pallas import tpu as pltpu
from jax.sharding import PartitionSpec as P

F32 = jnp.float32
VM = pl.BlockSpec(memory_space=pltpu.VMEM)
SM = pl.BlockSpec(memory_space=pltpu.SMEM)
ANY = pl.BlockSpec(memory_space=pl.ANY)
PARAMS = pltpu.CompilerParams(vmem_limit_bytes=44 * 2**20)
SMALL = pltpu.CompilerParams(vmem_limit_bytes=16 * 2**20)
LINES = 32
LINE = 8
PLANE = LINES * LINE
ROWS = LINES * PLANE
SPARE = 8
PARTS = 8
FINE = 16
AHEAD = 4
SPAN = ROWS // PARTS


def shape(rows):
    return pltpu.HBM((rows, 128), F32)


def in_hbm(*arrays):
    return [pltpu.with_memory_space_constraint(a, pltpu.HBM) for a in arrays]


def in_vmem(*arrays):
    return [pltpu.with_memory_space_constraint(a, pltpu.VMEM) for a in arrays]


def in_smem(*arrays):
    return [pltpu.with_memory_space_constraint(a, pltpu.SMEM) for a in arrays]


def tiles(a):
    x, y, z = a.shape
    return a.reshape(x, y // 8, 8, z // 128, 128).transpose(0, 1, 3, 2, 4).reshape(-1, 128)


def untiles(a, x, y, z):
    return a.reshape(x, y // 8, z // 128, 8, 128).transpose(0, 1, 3, 2, 4).reshape(x, y, z)


def aligned(i, n):
    return pl.multiple_of(i, n)


def tiled_line(x, y):
    return pl.ds(aligned(x * PLANE, PLANE) + (y // 8) * 64 + y % 8, LINE, stride=8)


def plain_line(x, y=0):
    return pl.ds(aligned(x * PLANE + y * LINE, LINE), LINE)


def place_in_tiles(r):
    return (r & ~63) | ((r & 7) << 3) | ((r >> 3) & 7)


def piece(ref, k, shift=0, parts=PARTS):
    return ref.at[pl.ds(aligned(k * (ROWS // parts) + shift, 8), ROWS // parts)]


def gather_kernel(rows, src, out, at, block, made, at_v, sems, done):
    loads = [pltpu.make_async_copy(piece(src, k), piece(block, k), sems.at[k]) for k in range(PARTS)]
    asked = pltpu.make_async_copy(rows, at_v, sems.at[PARTS])
    asked.start()
    for load in loads:
        load.start()
    asked.wait()
    at_v[...] = place_in_tiles(at_v[...])
    listed = pltpu.make_async_copy(at_v, at, sems.at[PARTS])
    listed.start()
    listed.wait()
    for load in loads:
        load.wait()
    groups = rows.shape[0]
    each = groups // PARTS

    def save(k):
        part = pl.ds(aligned(k * each * 128, 128), each * 128)
        return pltpu.make_async_copy(made.at[part], out.at[part], done.at[k])

    def step(k, _):
        def group(i, _):
            g = k * each + i
            base = aligned(g * 128, 128)
            for first in range(0, 128, 32):
                found = [block[pl.ds(at[g, first + n], 1), :] for n in range(32)]
                for n in range(32):
                    made[pl.ds(base + (first + n), 1), :] = found[n]
            return 0

        lax.fori_loop(0, each, group, 0)
        save(k).start()
        return 0

    lax.fori_loop(0, PARTS, step, 0)
    for k in range(PARTS):
        save(k).wait()


def gather(rows, src):
    n = rows.shape[0] * 128
    return pl.pallas_call(
        gather_kernel, out_shape=(shape(n), pltpu.SMEM(rows.shape, jnp.int32)),
        in_specs=[ANY, ANY], out_specs=(ANY, SM),
        scratch_shapes=[pltpu.VMEM((ROWS, 128), F32), pltpu.VMEM((n, 128), F32),
                        pltpu.VMEM(rows.shape, jnp.int32), pltpu.SemaphoreType.DMA((PARTS + 1,)),
                        pltpu.SemaphoreType.DMA((PARTS,))],
        compiler_params=PARAMS, name="gather_rows",
    )(*in_hbm(rows, src))


def finish_kernel(at, flux, src, kx0, kx1, ky0, ky1, xlo, xhi, ylo, yhi, out, block, sink, sides, sems, beside):
    loads = [pltpu.make_async_copy(piece(src, k), piece(block, k), sems.at[k]) for k in range(PARTS)]
    extra = [pltpu.make_async_copy(a, sides.at[n], beside.at[n])
             for n, a in enumerate((kx0, kx1, ky0, ky1, xlo, xhi, ylo, yhi))]
    for load in loads + extra:
        load.start()

    def clear(n, _):
        sink[pl.ds(aligned(n * PLANE, PLANE), PLANE), :] = jnp.zeros((PLANE, 128), F32)
        return 0

    lax.fori_loop(0, LINES, clear, 0)

    def group(g, _):
        base = aligned(g * 128, 128)
        for first in range(0, 128, 16):
            where = [at[g, first + n] for n in range(16)]
            rows = [flux[pl.ds(base + (first + n), 1), :] for n in range(16)]
            for t, v in zip(where, rows):
                sink[pl.ds(t, 1), :] = v
        return 0

    lax.fori_loop(0, at.shape[0], group, 0)
    for load in loads + extra:
        load.wait()
    for n in range(LINES):
        line = plain_line(0, n)
        for side, place in enumerate((tiled_line(0, n), tiled_line(LINES - 1, n),
                                      tiled_line(n, 0), tiled_line(n, LINES - 1))):
            block[place, :] = block[place, :] + sides[side, line, :] * sides[side + 4, line, :]

    def save(k):
        return pltpu.make_async_copy(piece(block, k), piece(out, k), sems.at[k])

    def step(k, _):
        def plane(i, _):
            part = pl.ds(aligned(k * SPAN + i * PLANE, PLANE), PLANE)
            block[part, :] = block[part, :] - sink[part, :]
            return 0

        lax.fori_loop(0, SPAN // PLANE, plane, 0)
        save(k).start()
        return 0

    lax.fori_loop(0, PARTS, step, 0)
    for k in range(PARTS):
        save(k).wait()


def finish(at, flux, src, gains, halos):
    return pl.pallas_call(
        finish_kernel, out_shape=shape(ROWS), in_specs=[SM, VM] + [ANY] * 9, out_specs=ANY,
        scratch_shapes=[pltpu.VMEM((ROWS + SPARE, 128), F32), pltpu.VMEM((ROWS, 128), F32),
                        pltpu.VMEM((8, PLANE, 128), F32),
                        pltpu.SemaphoreType.DMA((PARTS,)), pltpu.SemaphoreType.DMA((8,))],
        compiler_params=SMALL, name="subtract_rows",
    )(*in_smem(at), flux, *in_hbm(src, *gains, *halos))


def tie_kernel(*refs):
    pass


def after_all(array, others):
    n = len(others)
    return pl.pallas_call(
        tie_kernel, out_shape=pltpu.HBM(array.shape, array.dtype), in_specs=[VM] * n + [ANY], out_specs=ANY,
        input_output_aliases={n: 0}, compiler_params=SMALL, name="tie",
    )(*in_vmem(*others), *in_hbm(array))


def step_up(a, edge, corner, fill):
    rolled = pltpu.roll(a, 127, 1)
    carried = pltpu.roll(rolled, 7, 0)
    return jnp.where(edge, jnp.where(corner, fill, carried), rolled)


def step_down(a, edge, corner, fill):
    rolled = pltpu.roll(a, 1, 1)
    carried = pltpu.roll(rolled, 1, 0)
    return jnp.where(edge, jnp.where(corner, fill, carried), rolled)


def relax_plane(x, load_u, load_c, load_p, store, whole):
    lane = lax.broadcasted_iota(jnp.int32, (8, 128), 1)
    sub = lax.broadcasted_iota(jnp.int32, (8, 128), 0)
    top, bottom = lane == 127, lane == 0
    last, first = sub == 7, sub == 0
    zero = jnp.zeros((8, 128), F32)
    u_old, c_old, w_old = zero, zero, zero
    u, c = load_u(x, 0), load_c(x, 0)
    w = u * c
    for y in range(LINES):
        if y + 1 < LINES:
            u_new, c_new = load_u(x, y + 1), load_c(x, y + 1)
            w_new = u_new * c_new
        else:
            u_new, c_new, w_new = zero, zero, zero
        ul, uh = load_u(x - 1, y), load_u(x + 1, y)
        cl, ch = load_c(x - 1, y), load_c(x + 1, y)
        face = c + step_up(c, top, last, 0.0)
        flow = face * step_up(u, top, last, 0.0)
        back = step_down(face * u, bottom, first, 0.0)
        numer = c * ((u_old + u_new) + (ul + uh)) + ((w_old + w_new) + (cl * ul + ch * uh))
        numer = numer + (flow + back) + 2.0 * load_p(x, y)
        denom = None
        if whole:
            below = step_down(face, bottom, first, c)
            denom = 4.0 * c + ((c_old + c_new) + (cl + ch)) + (face + below)
        store(x, y, numer, denom, c)
        u_old, c_old, w_old = u, c, w
        u, c, w = u_new, c_new, w_new


def planes(start, ready, relax, after):
    each = LINES // FINE
    ready(0)

    def step(k, _):
        @pl.when(k + AHEAD < FINE)
        def _():
            start(k + AHEAD)

        @pl.when(k + 1 < FINE)
        def _():
            ready(k + 1)

        lax.fori_loop(0, each, lambda i, _: (relax(k * each + i), 0)[1], 0)
        after(k)
        return 0

    lax.fori_loop(0, FINE, step, 0)


def clear_beyond(*refs):
    for ref in refs:
        ref[pl.ds(0, PLANE), :] = jnp.zeros((PLANE, 128), F32)
        ref[pl.ds(PLANE + ROWS, PLANE), :] = jnp.zeros((PLANE, 128), F32)


def first_kernel(after, u, c, p, out, gain, sx0, sx1, sy0, sy1, us, cs, ps, vs, gs, sides, sems, done, sent):
    del after

    def loads(k):
        return [pltpu.make_async_copy(piece(a, k, 0, FINE), piece(b, k, shift, FINE), sems.at[n, k])
                for n, (a, b, shift) in enumerate(((u, us, PLANE), (c, cs, PLANE), (p, ps, 0)))]

    def saves(k):
        return [pltpu.make_async_copy(piece(a, k, 0, FINE), piece(b, k, 0, FINE), done.at[n, k])
                for n, (a, b) in enumerate(((vs, out), (gs, gain)))]

    for k in range(AHEAD):
        for load in loads(k):
            load.start()
    clear_beyond(us, cs)

    def start(k):
        for load in loads(k):
            load.start()

    load_u = lambda x, y: us[tiled_line(x + 1, y), :]
    load_c = lambda x, y: cs[tiled_line(x + 1, y), :]
    load_p = lambda x, y: ps[tiled_line(x, y), :]
    sends = [pltpu.make_async_copy(sides.at[n], ref, sent.at[n]) for n, ref in enumerate((sx0, sx1, sy0, sy1))]

    def ready(k):
        for load in loads(k):
            load.wait()

        @pl.when(k == FINE - 1)
        def _():
            for n in range(LINES):
                row, below = pl.ds(n * LINE, LINE), pl.ds(PLANE + n * LINE, LINE)
                for side, (x, y) in enumerate(((0, n), (LINES - 1, n), (n, 0), (n, LINES - 1))):
                    sides[side, row, :] = load_u(x, y)
                    sides[side, below, :] = load_c(x, y)
            for send in sends:
                send.start()

    def store(x, y, numer, denom, c):
        part = 1.0 / denom
        vs[plain_line(x, y), :] = numer * part
        gs[plain_line(x, y), :] = part

    def after_piece(k):
        for save in saves(k):
            save.start()

    planes(start, ready, lambda x: relax_plane(x, load_u, load_c, load_p, store, True), after_piece)
    for send in sends:
        send.wait()
    for k in range(FINE):
        for save in saves(k):
            save.wait()


def sweep_first(after, u, c, p):
    return pl.pallas_call(
        first_kernel, out_shape=(shape(ROWS),) * 2 + (shape(2 * PLANE),) * 4,
        in_specs=[ANY] * 4, out_specs=(ANY,) * 6,
        scratch_shapes=[pltpu.VMEM((ROWS + 2 * PLANE + SPARE, 128), F32), pltpu.VMEM((ROWS + 2 * PLANE + SPARE, 128), F32),
                        pltpu.VMEM((ROWS + SPARE, 128), F32), pltpu.VMEM((ROWS + SPARE, 128), F32),
                        pltpu.VMEM((ROWS + SPARE, 128), F32),
                        pltpu.VMEM((4, 2 * PLANE, 128), F32), pltpu.SemaphoreType.DMA((3, FINE)),
                        pltpu.SemaphoreType.DMA((2, FINE)), pltpu.SemaphoreType.DMA((4,))],
        compiler_params=PARAMS, name="sweep_first",
    )(*in_hbm(after, u, c, p))


def sides_kernel(after, once, gain, sx0, sx1, sy0, sy1, xlo, xhi, ylo, yhi, fx0, fx1, fy0, fy1,
                 bx0, bx1, by0, by1, on_x, on_y, cs, sems, passed):
    del after
    copies = []
    for n, a in enumerate((once, gain)):
        for side, x in enumerate((0, LINES - 1)):
            copies.append((a.at[x], on_x.at[n, side]))
            copies.append((a.at[:, pl.ds(x * LINE, LINE)], on_y.at[n, side]))
    for side, a in enumerate((sx0, sx1, sy0, sy1)):
        copies.append((a.at[pl.ds(PLANE, PLANE)], cs.at[side]))
    copies = [pltpu.make_async_copy(a, b, sems.at[n]) for n, (a, b) in enumerate(copies)]
    for copy in copies:
        copy.start()
    passing = [pltpu.make_async_copy(a.at[pl.ds(PLANE, PLANE)], b, passed.at[n])
               for n, (a, b) in enumerate(((xlo, bx0), (xhi, bx1), (ylo, by0), (yhi, by1)))]
    for copy in passing:
        copy.start()
    for copy in copies:
        copy.wait()
    end = PLANE - LINE
    for side, (ref, halo, ends) in enumerate((
        (fx0, xlo, ((ylo, 0), (yhi, 0))), (fx1, xhi, ((ylo, end), (yhi, end))),
        (fy0, ylo, ((xlo, 0), (xhi, 0))), (fy1, yhi, ((xlo, end), (xhi, end))),
    )):
        c = cs[side]
        v, g = [on_x[n, side] if side < 2 else on_y[n, side - 2].reshape(PLANE, 128) for n in range(2)]
        c_out = halo[pl.ds(PLANE, PLANE), :]
        numer = v + g * ((c + c_out) * halo[pl.ds(0, PLANE), :])
        denom = 1.0 + g * c_out
        ref[...] = numer / denom
        for start, (other, line) in zip((0, end), ends):
            at = slice(start, start + LINE)
            c_out = other[pl.ds(PLANE + line, LINE), :]
            more = numer[at] + g[at] * ((c[at] + c_out) * other[pl.ds(line, LINE), :])
            ref[pl.ds(start, LINE), :] = more / (denom[at] + g[at] * c_out)
    for copy in passing:
        copy.wait()


def fix_sides(after, once, gain, sides, halos):
    by_plane = lambda a: a.reshape(LINES, PLANE, 128)
    return pl.pallas_call(
        sides_kernel, out_shape=(shape(PLANE),) * 8, in_specs=[ANY] * 7 + [VM] * 4, out_specs=(VM,) * 4 + (ANY,) * 4,
        scratch_shapes=[pltpu.VMEM((2, 2, PLANE, 128), F32), pltpu.VMEM((2, 2, LINES, LINE, 128), F32),
                        pltpu.VMEM((4, PLANE, 128), F32), pltpu.SemaphoreType.DMA((12,)), pltpu.SemaphoreType.DMA((4,))],
        compiler_params=SMALL, name="sweep_first_sides",
    )(*in_hbm(after, by_plane(once), by_plane(gain), *sides), *in_vmem(*halos))


def second_kernel(after, u, c, p, gain, fx0, fx1, fy0, fy1, xlo, xhi, ylo, yhi, out, kx0, kx1, ky0, ky1,
                  us, cs, ps, gs, vs, sems, done):
    del after

    def loads(k):
        return [pltpu.make_async_copy(piece(a, k, 0, FINE), piece(b, k, shift, FINE), sems.at[n, k])
                for n, (a, b, shift) in enumerate(((u, us, PLANE), (c, cs, PLANE), (p, ps, 0), (gain, gs, 0)))]

    def save(k):
        return pltpu.make_async_copy(piece(vs, k, 0, FINE), piece(out, k, 0, FINE), done.at[k])

    for k in range(AHEAD):
        for load in loads(k):
            load.start()
    clear_beyond(us, cs)

    def start(k):
        for load in loads(k):
            load.start()

    def ready(k):
        for load in loads(k):
            load.wait()
        for i in range(LINES // FINE):
            x = k * (LINES // FINE) + i
            us[plain_line(x + 1, 0), :] = fy0[plain_line(0, x), :]
            us[plain_line(x + 1, LINES - 1), :] = fy1[plain_line(0, x), :]

        @pl.when(k == 0)
        def _():
            us[pl.ds(PLANE, PLANE), :] = fx0[...]

        @pl.when(k == FINE - 1)
        def _():
            us[pl.ds(ROWS, PLANE), :] = fx1[...]

    load_u = lambda x, y: us[plain_line(x + 1, y), :]
    load_c = lambda x, y: cs[tiled_line(x + 1, y), :]
    load_p = lambda x, y: ps[tiled_line(x, y), :]
    y_sides = {0: (ylo, ky0), LINES - 1: (yhi, ky1)}

    def beyond_y(x, y, part):
        outer = y_sides[y][0][plain_line(0, x), :]
        return outer, part / (1.0 + part * outer)

    def store(x, y, numer, _, c):
        part = gs[plain_line(x, y), :]
        if y in y_sides:
            outer, part = beyond_y(x, y, part)
            y_sides[y][1][plain_line(0, x), :] = (c + outer) * part
        vs[tiled_line(x, y), :] = numer * part

    def x_side(x, halo, k_side):
        for y in range(LINES):
            line = pl.ds(y * LINE, LINE)
            outer = halo[pl.ds(y * LINE, LINE), :]
            part = gs[plain_line(x, y), :]
            if y in y_sides:
                part = beyond_y(x, y, part)[1]
            less = 1.0 / (1.0 + part * outer)
            if y in y_sides:
                k_y = y_sides[y][1]
                k_y[plain_line(0, x), :] = k_y[plain_line(0, x), :] * less
            vs[tiled_line(x, y), :] = vs[tiled_line(x, y), :] * less
            k_side[line, :] = (load_c(x, y) + outer) * (part * less)

    def after_piece(k):
        @pl.when(k == 0)
        def _():
            x_side(0, xlo, kx0)

        @pl.when(k == FINE - 1)
        def _():
            x_side(LINES - 1, xhi, kx1)

        save(k).start()

    planes(start, ready, lambda x: relax_plane(x, load_u, load_c, load_p, store, False), after_piece)
    for k in range(FINE):
        save(k).wait()


def sweep_second(after, u, c, p, gain, faces, beyond):
    return pl.pallas_call(
        second_kernel, out_shape=(shape(ROWS),) + (shape(PLANE),) * 4,
        in_specs=[ANY] * 5 + [VM] * 8, out_specs=(ANY,) + (VM,) * 4,
        scratch_shapes=[pltpu.VMEM((ROWS + 2 * PLANE + SPARE, 128), F32), pltpu.VMEM((ROWS + 2 * PLANE + SPARE, 128), F32),
                        pltpu.VMEM((ROWS + SPARE, 128), F32), pltpu.VMEM((ROWS + SPARE, 128), F32),
                        pltpu.VMEM((ROWS + SPARE, 128), F32),
                        pltpu.SemaphoreType.DMA((4, FINE)), pltpu.SemaphoreType.DMA((FINE,))],
        compiler_params=PARAMS, name="sweep_second",
    )(*in_hbm(after, u, c, p, gain, *faces, *beyond))


def channel_kernel(*refs):
    (me, owners, arrived, props, carry, coef_at, inlet_at, fluid_out, flux_out,
     fluids, fluxes, weights, prev, coef, live, done_x, done_f, here_p) = refs[-18:]
    spans, groups = props.shape[0], arrived.shape[0]
    size = arrived.shape[1] // spans
    here = me[0]
    halves = [pltpu.make_async_copy(props.at[part], weights.at[part], here_p.at[n])
              for n, part in enumerate((pl.ds(0, spans // 2), pl.ds(spans // 2, spans // 2)))]
    for load in halves:
        load.start()
    owned = jnp.sum((owners[...] == here).astype(F32), axis=0, keepdims=True)
    owned = jnp.sum(owned, axis=1, keepdims=True)
    bf = jnp.bfloat16
    dot = functools.partial(jnp.dot, preferred_element_type=F32)

    def block(s):
        return pl.ds(aligned(lax.rem(here + s, spans) * size, size), size)

    def save_flux(s):
        return pltpu.make_async_copy(fluxes.at[:, block(s), :], flux_out.at[:, block(s), :], done_x.at[s])

    def save_fluid(n):
        part = pl.ds(n * 4 * groups, 4 * groups)
        return pltpu.make_async_copy(fluids.at[:, part, :], fluid_out.at[:, part, :], done_f.at[n])

    row = lax.broadcasted_iota(jnp.int32, (16, 128), 0)
    lane = lax.broadcasted_iota(jnp.int32, (16, 128), 1)
    for q in range(groups):
        mine = lane == row * groups + q
        for half in range(2):
            part = pl.ds(q * size + half * 16, 16)
            for ref, values in ((prev, inlet_at), (coef, coef_at)):
                column = jnp.sum(jnp.where(mine, values[pl.ds(half, 1), :], 0.0), axis=1, keepdims=True)
                ref[part, :] = jnp.broadcast_to(column, (16, 128))
            live[part, :] = jnp.where(((row + half * 16) * groups + q).astype(F32) < owned, 1.0, 0.0)
    keep = live[...] > 0.0

    for s in range(spans):
        if s % (spans // 2) == 0:
            halves[s // (spans // 2)].wait()
        turn = lax.div(here + s, spans)
        at = [(lax.rem(turn + q, groups), block(s)) for q in range(groups)]
        wall = jnp.concatenate([arrived[g, r, :] for g, r in at], axis=0)
        scale = coef[...]
        x = scale * wall
        hi = x.astype(bf)
        lo = (x - hi.astype(F32)).astype(bf)
        p = weights[s]
        p_hi = p.astype(bf)
        p_lo = (p - p_hi.astype(F32)).astype(bf)
        fresh = (dot(lo, p_hi) + dot(hi, p_lo)) + dot(hi, p_hi)
        fluid = fresh + carry[pl.ds(s, 1), :] * prev[...]
        if s + 1 < spans:
            prev[...] = jnp.broadcast_to(fluid[:, 127:128], fluid.shape)
        flux = jnp.where(keep, scale * (wall - fluid), 0.0)
        fluid = jnp.where(keep, fluid, 0.0)
        for q, (g, r) in enumerate(at):
            fluxes[g, r, :] = flux[q * size:(q + 1) * size]
            fluids[:, s * groups + q, :] = fluid[q * size:(q + 1) * size]
        save_flux(s).start()
        if s % 4 == 3:
            save_fluid(s // 4).start()
    for s in range(spans):
        save_flux(s).wait()
    for n in range(spans // 4):
        save_fluid(n).wait()


def channel(after, me, owners, arrived, props, carry, coef, inlet):
    spans = props.shape[0]
    groups = 8
    size = coef.shape[0] // groups
    rows = spans * size
    fluid, flux = pl.pallas_call(
        channel_kernel,
        out_shape=(jax.ShapeDtypeStruct((size, spans * groups, 128), F32),
                   pltpu.HBM((groups, rows, 128), F32)),
        in_specs=[ANY] * len(after) + [SM] + [VM] * 2 + [ANY] + [VM] * 3, out_specs=(ANY, ANY),
        scratch_shapes=[pltpu.VMEM((size, (spans + 1) * groups, 128), F32), pltpu.VMEM((groups, rows, 128), F32),
                        pltpu.VMEM(props.shape, F32)]
        + [pltpu.VMEM((groups * size, 128), F32)] * 3
        + [pltpu.SemaphoreType.DMA((spans,)), pltpu.SemaphoreType.DMA((spans // 4,)),
           pltpu.SemaphoreType.DMA((2,))],
        compiler_params=SMALL, name="channel_march",
    )(*in_hbm(*after), me, owners, arrived.reshape(groups, rows, 128), *in_hbm(props), carry,
      coef.reshape(2, 128), inlet.reshape(2, 128))
    return fluid.reshape(-1, 128), flux


def up(a, axis):
    n = lax.axis_size(axis)
    return lax.ppermute(a, axis, [(i, i + 1) for i in range(n - 1)])


def down(a, axis):
    n = lax.axis_size(axis)
    return lax.ppermute(a, axis, [(i + 1, i) for i in range(n - 1)])


def local(solid_temp, conduct, power, channel_owner, wall_rows, span_prop, span_carry,
          channel_coef, channel_inlet):
    both = ("gx", "gy")
    devices = lax.axis_size(both)
    me = lax.axis_index(both).astype(jnp.int32).reshape(1)
    slots = channel_coef.shape[0]
    u, c, p = tiles(solid_temp), tiles(conduct), tiles(power)

    sent, at = gather(wall_rows.reshape(-1, 128), u)
    arrived = lax.all_to_all(sent.reshape(devices, -1, 128), both, 0, 0, tiled=True)

    once, gain, *sides = sweep_first(sent, u, c, p)
    halos = (up(sides[1], "gx"), down(sides[0], "gx"), up(sides[3], "gy"), down(sides[2], "gy"))

    fluid, flux = channel((once,), me, channel_owner.reshape(-1, 128), arrived, span_prop, span_carry,
                          channel_coef, channel_inlet)
    flux = after_all(flux, halos)
    returned = lax.all_to_all(flux.reshape(devices, -1, 128), both, 0, 0, tiled=True)

    faces = fix_sides(flux, once, gain, sides, halos)
    faces, beyond = faces[:4], faces[4:]
    outer = (up(faces[1], "gx"), down(faces[0], "gx"), up(faces[3], "gy"), down(faces[2], "gy"))
    twice, *gains = sweep_second(flux, once, c, p, gain, faces, beyond)
    solid_out = finish(at, returned.reshape(-1, 128), twice, gains, outer)
    return untiles(solid_out, *solid_temp.shape), untiles(fluid, 1, slots, span_carry.shape[0] * 128)[0]


def solution(mesh):
    both = ("gx", "gy")
    placed = (P("gx", "gy", None),) * 3 + (P(),) + (P(both),) + (
        P(both, None, None), P(both, None), P(both), P(both))
    return jax.shard_map(local, mesh=mesh, in_specs=placed,
                         out_specs=(P("gx", "gy", None), P(both, None)), check_vma=False)
```

```python
import functools

import jax
import jax.numpy as jnp
from jax import lax
from jax.experimental import pallas as pl
from jax.experimental.pallas import tpu as pltpu
from jax.sharding import PartitionSpec as P

F32 = jnp.float32
GY = ("pair", "core")
VM = pl.BlockSpec(memory_space=pltpu.VMEM)
SM = pl.BlockSpec(memory_space=pltpu.SMEM)
ANY = pl.BlockSpec(memory_space=pl.ANY)
PARAMS = pltpu.CompilerParams(vmem_limit_bytes=44 * 2**20)
SMALL = pltpu.CompilerParams(vmem_limit_bytes=16 * 2**20)
LINES = 32
LINE = 8
PLANE = LINES * LINE
ROWS = LINES * PLANE
SPARE = 8
PARTS = 8
FINE = 16
AHEAD = 4
SPAN = ROWS // PARTS


def shape(rows):
    return pltpu.HBM((rows, 128), F32)


def in_hbm(*arrays):
    return [pltpu.with_memory_space_constraint(a, pltpu.HBM) for a in arrays]


def in_vmem(*arrays):
    return [pltpu.with_memory_space_constraint(a, pltpu.VMEM) for a in arrays]


def in_smem(*arrays):
    return [pltpu.with_memory_space_constraint(a, pltpu.SMEM) for a in arrays]


def tiles(a):
    x, y, z = a.shape
    return a.reshape(x, y // 8, 8, z // 128, 128).transpose(0, 1, 3, 2, 4).reshape(-1, 128)


def untiles(a, x, y, z):
    return a.reshape(x, y // 8, z // 128, 8, 128).transpose(0, 1, 3, 2, 4).reshape(x, y, z)


def aligned(i, n):
    return pl.multiple_of(i, n)


def tiled_line(x, y):
    return pl.ds(aligned(x * PLANE, PLANE) + (y // 8) * 64 + y % 8, LINE, stride=8)


def plain_line(x, y=0):
    return pl.ds(aligned(x * PLANE + y * LINE, LINE), LINE)


def place_in_tiles(r):
    return (r & ~63) | ((r & 7) << 3) | ((r >> 3) & 7)


def piece(ref, k, shift=0, parts=PARTS):
    return ref.at[pl.ds(aligned(k * (ROWS // parts) + shift, 8), ROWS // parts)]


def order_by_core(lists):
    half = lists.shape[0] // 2
    even, odd = lists[pl.ds(0, half, stride=2), :], lists[pl.ds(1, half, stride=2), :]
    lane = lax.broadcasted_iota(jnp.int32, (half, 128), 1)

    def four(*parts):
        return jnp.where(lane < 32, parts[0], jnp.where(lane < 64, parts[1], jnp.where(lane < 96, parts[2], parts[3])))

    turned = lambda a, n: pltpu.roll(a, n, 1)
    lists[pl.ds(0, half), :] = four(even, turned(even, 96), turned(odd, 64), turned(odd, 32))
    lists[pl.ds(half, half), :] = four(turned(even, 96), turned(even, 64), turned(odd, 32), odd)


def gather_kernel(rows, src, out, at, block, made, at_v, sems, done):
    loads = [pltpu.make_async_copy(piece(src, k), piece(block, k), sems.at[k]) for k in range(PARTS)]
    asked = pltpu.make_async_copy(rows, at_v, sems.at[PARTS])
    asked.start()
    for load in loads:
        load.start()
    asked.wait()
    at_v[...] = place_in_tiles(at_v[...])
    order_by_core(at_v)
    listed = pltpu.make_async_copy(at_v, at, sems.at[PARTS])
    listed.start()
    listed.wait()
    for load in loads:
        load.wait()
    groups = rows.shape[0]
    each = groups // PARTS

    def save(k):
        part = pl.ds(aligned(k * each * 128, 128), each * 128)
        return pltpu.make_async_copy(made.at[part], out.at[part], done.at[k])

    def step(k, _):
        def group(i, _):
            g = k * each + i
            base = aligned(g * 128, 128)
            for first in range(0, 128, 32):
                found = [block[pl.ds(at[g, first + n], 1), :] for n in range(32)]
                for n in range(32):
                    made[pl.ds(base + (first + n), 1), :] = found[n]
            return 0

        lax.fori_loop(0, each, group, 0)
        save(k).start()
        return 0

    lax.fori_loop(0, PARTS, step, 0)
    for k in range(PARTS):
        save(k).wait()


def gather(rows, src):
    n = rows.shape[0] * 128
    return pl.pallas_call(
        gather_kernel, out_shape=(shape(n), pltpu.SMEM(rows.shape, jnp.int32)),
        in_specs=[ANY, ANY], out_specs=(ANY, SM),
        scratch_shapes=[pltpu.VMEM((ROWS, 128), F32), pltpu.VMEM((n, 128), F32),
                        pltpu.VMEM(rows.shape, jnp.int32), pltpu.SemaphoreType.DMA((PARTS + 1,)),
                        pltpu.SemaphoreType.DMA((PARTS,))],
        compiler_params=PARAMS, name="gather_rows",
    )(*in_hbm(rows, src))


def finish_kernel(at, flux, src, kx0, kx1, ky0, ky1, xlo, xhi, ylo, yhi, out, block, sink, sides, sems, beside):
    loads = [pltpu.make_async_copy(piece(src, k), piece(block, k), sems.at[k]) for k in range(PARTS)]
    extra = [pltpu.make_async_copy(a, sides.at[n], beside.at[n])
             for n, a in enumerate((kx0, kx1, ky0, ky1, xlo, xhi, ylo, yhi))]
    for load in loads + extra:
        load.start()

    def clear(n, _):
        sink[pl.ds(aligned(n * PLANE, PLANE), PLANE), :] = jnp.zeros((PLANE, 128), F32)
        return 0

    lax.fori_loop(0, LINES, clear, 0)

    def group(g, _):
        base = aligned(g * 128, 128)
        for first in range(0, 128, 16):
            where = [at[g, first + n] for n in range(16)]
            rows = [flux[pl.ds(base + (first + n), 1), :] for n in range(16)]
            for t, v in zip(where, rows):
                sink[pl.ds(t, 1), :] = v
        return 0

    lax.fori_loop(0, at.shape[0], group, 0)
    for load in loads + extra:
        load.wait()
    for n in range(LINES):
        line = plain_line(0, n)
        for side, place in enumerate((tiled_line(0, n), tiled_line(LINES - 1, n),
                                      tiled_line(n, 0), tiled_line(n, LINES - 1))):
            block[place, :] = block[place, :] + sides[side, line, :] * sides[side + 4, line, :]

    def save(k):
        return pltpu.make_async_copy(piece(block, k), piece(out, k), sems.at[k])

    def step(k, _):
        def plane(i, _):
            part = pl.ds(aligned(k * SPAN + i * PLANE, PLANE), PLANE)
            block[part, :] = block[part, :] - sink[part, :]
            return 0

        lax.fori_loop(0, SPAN // PLANE, plane, 0)
        save(k).start()
        return 0

    lax.fori_loop(0, PARTS, step, 0)
    for k in range(PARTS):
        save(k).wait()


def finish(at, flux, src, gains, halos):
    return pl.pallas_call(
        finish_kernel, out_shape=shape(ROWS), in_specs=[SM, VM] + [ANY] * 9, out_specs=ANY,
        scratch_shapes=[pltpu.VMEM((ROWS + SPARE, 128), F32), pltpu.VMEM((ROWS, 128), F32),
                        pltpu.VMEM((8, PLANE, 128), F32),
                        pltpu.SemaphoreType.DMA((PARTS,)), pltpu.SemaphoreType.DMA((8,))],
        compiler_params=SMALL, name="subtract_rows",
    )(*in_smem(at), flux, *in_hbm(src, *gains, *halos))


def tie_kernel(*refs):
    pass


def after_all(array, others):
    n = len(others)
    return pl.pallas_call(
        tie_kernel, out_shape=pltpu.HBM(array.shape, array.dtype), in_specs=[VM] * n + [ANY], out_specs=ANY,
        input_output_aliases={n: 0}, compiler_params=SMALL, name="tie",
    )(*in_vmem(*others), *in_hbm(array))


def step_up(a, edge, corner, fill):
    rolled = pltpu.roll(a, 127, 1)
    carried = pltpu.roll(rolled, 7, 0)
    return jnp.where(edge, jnp.where(corner, fill, carried), rolled)


def step_down(a, edge, corner, fill):
    rolled = pltpu.roll(a, 1, 1)
    carried = pltpu.roll(rolled, 1, 0)
    return jnp.where(edge, jnp.where(corner, fill, carried), rolled)


def relax_plane(x, load_u, load_c, load_p, store, whole):
    lane = lax.broadcasted_iota(jnp.int32, (8, 128), 1)
    sub = lax.broadcasted_iota(jnp.int32, (8, 128), 0)
    top, bottom = lane == 127, lane == 0
    last, first = sub == 7, sub == 0
    zero = jnp.zeros((8, 128), F32)
    u_old, c_old, w_old = zero, zero, zero
    u, c = load_u(x, 0), load_c(x, 0)
    w = u * c
    for y in range(LINES):
        if y + 1 < LINES:
            u_new, c_new = load_u(x, y + 1), load_c(x, y + 1)
            w_new = u_new * c_new
        else:
            u_new, c_new, w_new = zero, zero, zero
        ul, uh = load_u(x - 1, y), load_u(x + 1, y)
        cl, ch = load_c(x - 1, y), load_c(x + 1, y)
        face = c + step_up(c, top, last, 0.0)
        flow = face * step_up(u, top, last, 0.0)
        back = step_down(face * u, bottom, first, 0.0)
        numer = c * ((u_old + u_new) + (ul + uh)) + ((w_old + w_new) + (cl * ul + ch * uh))
        numer = numer + (flow + back) + 2.0 * load_p(x, y)
        denom = None
        if whole:
            below = step_down(face, bottom, first, c)
            denom = 4.0 * c + ((c_old + c_new) + (cl + ch)) + (face + below)
        store(x, y, numer, denom, c)
        u_old, c_old, w_old = u, c, w
        u, c, w = u_new, c_new, w_new


def planes(start, ready, relax, after):
    each = LINES // FINE
    ready(0)

    def step(k, _):
        @pl.when(k + AHEAD < FINE)
        def _():
            start(k + AHEAD)

        @pl.when(k + 1 < FINE)
        def _():
            ready(k + 1)

        lax.fori_loop(0, each, lambda i, _: (relax(k * each + i), 0)[1], 0)
        after(k)
        return 0

    lax.fori_loop(0, FINE, step, 0)


def clear_beyond(*refs):
    for ref in refs:
        ref[pl.ds(0, PLANE), :] = jnp.zeros((PLANE, 128), F32)
        ref[pl.ds(PLANE + ROWS, PLANE), :] = jnp.zeros((PLANE, 128), F32)


def first_kernel(after, u, c, p, out, gain, sx0, sx1, sy0, sy1, us, cs, ps, vs, gs, sides, sems, done, sent):
    del after

    def loads(k):
        return [pltpu.make_async_copy(piece(a, k, 0, FINE), piece(b, k, shift, FINE), sems.at[n, k])
                for n, (a, b, shift) in enumerate(((u, us, PLANE), (c, cs, PLANE), (p, ps, 0)))]

    def saves(k):
        return [pltpu.make_async_copy(piece(a, k, 0, FINE), piece(b, k, 0, FINE), done.at[n, k])
                for n, (a, b) in enumerate(((vs, out), (gs, gain)))]

    for k in range(AHEAD):
        for load in loads(k):
            load.start()
    clear_beyond(us, cs)

    def start(k):
        for load in loads(k):
            load.start()

    load_u = lambda x, y: us[tiled_line(x + 1, y), :]
    load_c = lambda x, y: cs[tiled_line(x + 1, y), :]
    load_p = lambda x, y: ps[tiled_line(x, y), :]
    sends = [pltpu.make_async_copy(sides.at[n], ref, sent.at[n]) for n, ref in enumerate((sx0, sx1, sy0, sy1))]

    def ready(k):
        for load in loads(k):
            load.wait()

        @pl.when(k == FINE - 1)
        def _():
            for n in range(LINES):
                row, below = pl.ds(n * LINE, LINE), pl.ds(PLANE + n * LINE, LINE)
                for side, (x, y) in enumerate(((0, n), (LINES - 1, n), (n, 0), (n, LINES - 1))):
                    sides[side, row, :] = load_u(x, y)
                    sides[side, below, :] = load_c(x, y)
            for send in sends:
                send.start()

    def store(x, y, numer, denom, c):
        part = 1.0 / denom
        vs[plain_line(x, y), :] = numer * part
        gs[plain_line(x, y), :] = part

    def after_piece(k):
        for save in saves(k):
            save.start()

    planes(start, ready, lambda x: relax_plane(x, load_u, load_c, load_p, store, True), after_piece)
    for send in sends:
        send.wait()
    for k in range(FINE):
        for save in saves(k):
            save.wait()


def sweep_first(after, u, c, p):
    return pl.pallas_call(
        first_kernel, out_shape=(shape(ROWS),) * 2 + (shape(2 * PLANE),) * 4,
        in_specs=[ANY] * 4, out_specs=(ANY,) * 6,
        scratch_shapes=[pltpu.VMEM((ROWS + 2 * PLANE + SPARE, 128), F32), pltpu.VMEM((ROWS + 2 * PLANE + SPARE, 128), F32),
                        pltpu.VMEM((ROWS + SPARE, 128), F32), pltpu.VMEM((ROWS + SPARE, 128), F32),
                        pltpu.VMEM((ROWS + SPARE, 128), F32),
                        pltpu.VMEM((4, 2 * PLANE, 128), F32), pltpu.SemaphoreType.DMA((3, FINE)),
                        pltpu.SemaphoreType.DMA((2, FINE)), pltpu.SemaphoreType.DMA((4,))],
        compiler_params=PARAMS, name="sweep_first",
    )(*in_hbm(after, u, c, p))


def sides_kernel(after, once, gain, sx0, sx1, sy0, sy1, xlo, xhi, ylo, yhi, fx0, fx1, fy0, fy1,
                 bx0, bx1, by0, by1, on_x, on_y, cs, sems, passed):
    del after
    copies = []
    for n, a in enumerate((once, gain)):
        for side, x in enumerate((0, LINES - 1)):
            copies.append((a.at[x], on_x.at[n, side]))
            copies.append((a.at[:, pl.ds(x * LINE, LINE)], on_y.at[n, side]))
    for side, a in enumerate((sx0, sx1, sy0, sy1)):
        copies.append((a.at[pl.ds(PLANE, PLANE)], cs.at[side]))
    copies = [pltpu.make_async_copy(a, b, sems.at[n]) for n, (a, b) in enumerate(copies)]
    for copy in copies:
        copy.start()
    passing = [pltpu.make_async_copy(a.at[pl.ds(PLANE, PLANE)], b, passed.at[n])
               for n, (a, b) in enumerate(((xlo, bx0), (xhi, bx1), (ylo, by0), (yhi, by1)))]
    for copy in passing:
        copy.start()
    for copy in copies:
        copy.wait()
    end = PLANE - LINE
    for side, (ref, halo, ends) in enumerate((
        (fx0, xlo, ((ylo, 0), (yhi, 0))), (fx1, xhi, ((ylo, end), (yhi, end))),
        (fy0, ylo, ((xlo, 0), (xhi, 0))), (fy1, yhi, ((xlo, end), (xhi, end))),
    )):
        c = cs[side]
        v, g = [on_x[n, side] if side < 2 else on_y[n, side - 2].reshape(PLANE, 128) for n in range(2)]
        c_out = halo[pl.ds(PLANE, PLANE), :]
        numer = v + g * ((c + c_out) * halo[pl.ds(0, PLANE), :])
        denom = 1.0 + g * c_out
        ref[...] = numer / denom
        for start, (other, line) in zip((0, end), ends):
            at = slice(start, start + LINE)
            c_out = other[pl.ds(PLANE + line, LINE), :]
            more = numer[at] + g[at] * ((c[at] + c_out) * other[pl.ds(line, LINE), :])
            ref[pl.ds(start, LINE), :] = more / (denom[at] + g[at] * c_out)
    for copy in passing:
        copy.wait()


def fix_sides(after, once, gain, sides, halos):
    by_plane = lambda a: a.reshape(LINES, PLANE, 128)
    return pl.pallas_call(
        sides_kernel, out_shape=(shape(PLANE),) * 8, in_specs=[ANY] * 7 + [VM] * 4, out_specs=(VM,) * 4 + (ANY,) * 4,
        scratch_shapes=[pltpu.VMEM((2, 2, PLANE, 128), F32), pltpu.VMEM((2, 2, LINES, LINE, 128), F32),
                        pltpu.VMEM((4, PLANE, 128), F32), pltpu.SemaphoreType.DMA((12,)), pltpu.SemaphoreType.DMA((4,))],
        compiler_params=SMALL, name="sweep_first_sides",
    )(*in_hbm(after, by_plane(once), by_plane(gain), *sides), *in_vmem(*halos))


def second_kernel(after, u, c, p, gain, fx0, fx1, fy0, fy1, xlo, xhi, ylo, yhi, out, kx0, kx1, ky0, ky1,
                  us, cs, ps, gs, vs, sems, done):
    del after

    def loads(k):
        return [pltpu.make_async_copy(piece(a, k, 0, FINE), piece(b, k, shift, FINE), sems.at[n, k])
                for n, (a, b, shift) in enumerate(((u, us, PLANE), (c, cs, PLANE), (p, ps, 0), (gain, gs, 0)))]

    def save(k):
        return pltpu.make_async_copy(piece(vs, k, 0, FINE), piece(out, k, 0, FINE), done.at[k])

    for k in range(AHEAD):
        for load in loads(k):
            load.start()
    clear_beyond(us, cs)

    def start(k):
        for load in loads(k):
            load.start()

    def ready(k):
        for load in loads(k):
            load.wait()
        for i in range(LINES // FINE):
            x = k * (LINES // FINE) + i
            us[plain_line(x + 1, 0), :] = fy0[plain_line(0, x), :]
            us[plain_line(x + 1, LINES - 1), :] = fy1[plain_line(0, x), :]

        @pl.when(k == 0)
        def _():
            us[pl.ds(PLANE, PLANE), :] = fx0[...]

        @pl.when(k == FINE - 1)
        def _():
            us[pl.ds(ROWS, PLANE), :] = fx1[...]

    load_u = lambda x, y: us[plain_line(x + 1, y), :]
    load_c = lambda x, y: cs[tiled_line(x + 1, y), :]
    load_p = lambda x, y: ps[tiled_line(x, y), :]
    y_sides = {0: (ylo, ky0), LINES - 1: (yhi, ky1)}

    def beyond_y(x, y, part):
        outer = y_sides[y][0][plain_line(0, x), :]
        return outer, part / (1.0 + part * outer)

    def store(x, y, numer, _, c):
        part = gs[plain_line(x, y), :]
        if y in y_sides:
            outer, part = beyond_y(x, y, part)
            y_sides[y][1][plain_line(0, x), :] = (c + outer) * part
        vs[tiled_line(x, y), :] = numer * part

    def x_side(x, halo, k_side):
        for y in range(LINES):
            line = pl.ds(y * LINE, LINE)
            outer = halo[pl.ds(y * LINE, LINE), :]
            part = gs[plain_line(x, y), :]
            if y in y_sides:
                part = beyond_y(x, y, part)[1]
            less = 1.0 / (1.0 + part * outer)
            if y in y_sides:
                k_y = y_sides[y][1]
                k_y[plain_line(0, x), :] = k_y[plain_line(0, x), :] * less
            vs[tiled_line(x, y), :] = vs[tiled_line(x, y), :] * less
            k_side[line, :] = (load_c(x, y) + outer) * (part * less)

    def after_piece(k):
        @pl.when(k == 0)
        def _():
            x_side(0, xlo, kx0)

        @pl.when(k == FINE - 1)
        def _():
            x_side(LINES - 1, xhi, kx1)

        save(k).start()

    planes(start, ready, lambda x: relax_plane(x, load_u, load_c, load_p, store, False), after_piece)
    for k in range(FINE):
        save(k).wait()


def sweep_second(after, u, c, p, gain, faces, beyond):
    return pl.pallas_call(
        second_kernel, out_shape=(shape(ROWS),) + (shape(PLANE),) * 4,
        in_specs=[ANY] * 5 + [VM] * 8, out_specs=(ANY,) + (VM,) * 4,
        scratch_shapes=[pltpu.VMEM((ROWS + 2 * PLANE + SPARE, 128), F32), pltpu.VMEM((ROWS + 2 * PLANE + SPARE, 128), F32),
                        pltpu.VMEM((ROWS + SPARE, 128), F32), pltpu.VMEM((ROWS + SPARE, 128), F32),
                        pltpu.VMEM((ROWS + SPARE, 128), F32),
                        pltpu.SemaphoreType.DMA((4, FINE)), pltpu.SemaphoreType.DMA((FINE,))],
        compiler_params=PARAMS, name="sweep_second",
    )(*in_hbm(after, u, c, p, gain, *faces, *beyond))


def channel_kernel(*refs):
    (me, owners, arrived, props, carry, coef_at, inlet_at, fluid_out, flux_out,
     fluids, fluxes, weights, prev, coef, live, done_x, done_f, here_p) = refs[-18:]
    spans, groups = props.shape[0], arrived.shape[0] // 2
    size = arrived.shape[1] // groups
    here = me[0]
    halves = [pltpu.make_async_copy(props.at[part], weights.at[part], here_p.at[n])
              for n, part in enumerate((pl.ds(0, spans // 2), pl.ds(spans // 2, spans // 2)))]
    for load in halves:
        load.start()
    owned = jnp.sum((owners[...] == here).astype(F32), axis=0, keepdims=True)
    owned = jnp.sum(owned, axis=1, keepdims=True)
    bf = jnp.bfloat16
    dot = functools.partial(jnp.dot, preferred_element_type=F32)

    def block(s):
        return pl.ds(aligned(lax.rem(lax.div(here + s, 2), groups) * size, size), size)

    def core(s):
        return lax.rem(here + s, 2) * groups

    def save_flux(s):
        return pltpu.make_async_copy(fluxes.at[pl.ds(core(s), groups), block(s), :], flux_out.at[pl.ds(core(s), groups), block(s), :], done_x.at[s])

    def save_fluid(n):
        part = pl.ds(n * 4 * groups, 4 * groups)
        return pltpu.make_async_copy(fluids.at[:, part, :], fluid_out.at[:, part, :], done_f.at[n])

    row = lax.broadcasted_iota(jnp.int32, (16, 128), 0)
    lane = lax.broadcasted_iota(jnp.int32, (16, 128), 1)
    for q in range(groups):
        mine = lane == row * groups + q
        for half in range(2):
            part = pl.ds(q * size + half * 16, 16)
            for ref, values in ((prev, inlet_at), (coef, coef_at)):
                column = jnp.sum(jnp.where(mine, values[pl.ds(half, 1), :], 0.0), axis=1, keepdims=True)
                ref[part, :] = jnp.broadcast_to(column, (16, 128))
            live[part, :] = jnp.where(((row + half * 16) * groups + q).astype(F32) < owned, 1.0, 0.0)
    keep = live[...] > 0.0

    for s in range(spans):
        if s % (spans // 2) == 0:
            halves[s // (spans // 2)].wait()
        turn = lax.div(here + s, spans)
        at = [(core(s) + lax.rem(turn + q, groups), block(s)) for q in range(groups)]
        wall = jnp.concatenate([arrived[g, r, :] for g, r in at], axis=0)
        scale = coef[...]
        x = scale * wall
        hi = x.astype(bf)
        lo = (x - hi.astype(F32)).astype(bf)
        p = weights[s]
        p_hi = p.astype(bf)
        p_lo = (p - p_hi.astype(F32)).astype(bf)
        fresh = (dot(lo, p_hi) + dot(hi, p_lo)) + dot(hi, p_hi)
        fluid = fresh + carry[pl.ds(s, 1), :] * prev[...]
        if s + 1 < spans:
            prev[...] = jnp.broadcast_to(fluid[:, 127:128], fluid.shape)
        flux = jnp.where(keep, scale * (wall - fluid), 0.0)
        fluid = jnp.where(keep, fluid, 0.0)
        for q, (g, r) in enumerate(at):
            fluxes[g, r, :] = flux[q * size:(q + 1) * size]
            fluids[:, s * groups + q, :] = fluid[q * size:(q + 1) * size]
        save_flux(s).start()
        if s % 4 == 3:
            save_fluid(s // 4).start()
    for s in range(spans):
        save_flux(s).wait()
    for n in range(spans // 4):
        save_fluid(n).wait()


def channel(after, me, owners, arrived, props, carry, coef, inlet):
    spans = props.shape[0]
    groups = 8
    size = coef.shape[0] // groups
    rows = groups * size
    fluid, flux = pl.pallas_call(
        channel_kernel,
        out_shape=(jax.ShapeDtypeStruct((size, spans * groups, 128), F32),
                   pltpu.HBM((2 * groups, rows, 128), F32)),
        in_specs=[ANY] * len(after) + [SM] + [VM] * 2 + [ANY] + [VM] * 3, out_specs=(ANY, ANY),
        scratch_shapes=[pltpu.VMEM((size, (spans + 1) * groups, 128), F32), pltpu.VMEM((2 * groups, rows, 128), F32),
                        pltpu.VMEM(props.shape, F32)]
        + [pltpu.VMEM((groups * size, 128), F32)] * 3
        + [pltpu.SemaphoreType.DMA((spans,)), pltpu.SemaphoreType.DMA((spans // 4,)),
           pltpu.SemaphoreType.DMA((2,))],
        compiler_params=SMALL, name="channel_march",
    )(*in_hbm(*after), me, owners, arrived.reshape(2 * groups, rows, 128), *in_hbm(props), carry,
      coef.reshape(2, 128), inlet.reshape(2, 128))
    return fluid.reshape(-1, 128), flux


def up(a, axis):
    n = lax.axis_size(axis)
    return lax.ppermute(a, axis, [(i, i + 1) for i in range(n - 1)])


def down(a, axis):
    n = lax.axis_size(axis)
    return lax.ppermute(a, axis, [(i + 1, i) for i in range(n - 1)])


def local(solid_temp, conduct, power, channel_owner, wall_rows, span_prop, span_carry,
          channel_coef, channel_inlet):
    both = ("gx", *GY)
    by_core = ("core", "gx", "pair")
    devices = lax.axis_size(both)
    me = lax.axis_index(both).astype(jnp.int32).reshape(1)
    slots = channel_coef.shape[0]
    u, c, p = tiles(solid_temp), tiles(conduct), tiles(power)

    sent, at = gather(wall_rows.reshape(-1, 128), u)
    arrived = lax.all_to_all(sent.reshape(devices, -1, 128), by_core, 0, 0, tiled=True)

    once, gain, *sides = sweep_first(sent, u, c, p)
    halos = (up(sides[1], "gx"), down(sides[0], "gx"), up(sides[3], GY), down(sides[2], GY))

    fluid, flux = channel((once,), me, channel_owner.reshape(-1, 128), arrived, span_prop, span_carry,
                          channel_coef, channel_inlet)
    flux = after_all(flux, halos)
    returned = lax.all_to_all(flux.reshape(devices, -1, 128), by_core, 0, 0, tiled=True)

    faces = fix_sides(flux, once, gain, sides, halos)
    faces, beyond = faces[:4], faces[4:]
    outer = (up(faces[1], "gx"), down(faces[0], "gx"), up(faces[3], GY), down(faces[2], GY))
    twice, *gains = sweep_second(flux, once, c, p, gain, faces, beyond)
    solid_out = finish(at, returned.reshape(-1, 128), twice, gains, outer)
    return untiles(solid_out, *solid_temp.shape), untiles(fluid, 1, slots, span_carry.shape[0] * 128)[0]


def solution(mesh):
    split = jax.sharding.Mesh(mesh.devices.reshape(mesh.shape["gx"], -1, 2), ("gx", *GY))
    both = ("gx", *GY)
    placed = (P("gx", GY, None),) * 3 + (P(),) + (P(both),) + (
        P(both, None, None), P(both, None), P(both), P(both))
    return jax.shard_map(local, mesh=split, in_specs=placed,
                         out_specs=(P("gx", GY, None), P(both, None)), check_vma=False)
```
